1024 devices in a mesh: group: 16 (over y_hi, x, core), dom: 64 (over z, y_lo).
Axes of the slice: x: 4, y: 8 (y_hi: 2, y_lo: 4; y = y_hi * 4 + y_lo), z: 16, core: 2. Of those that a mesh axis runs over, the one named last changes fastest.
Arguments:
- u_prev: float32 [3, 2048, 2048], P(None, 'dom', 'group'), may hold values from -6 to 6
- u_now: float32 [3, 2048, 2048], P(None, 'dom', 'group'), may hold values from -6 to 6
- memory: float32 [3, 3, 2048, 2048], P(None, None, 'dom', 'group'), may hold values from -4 to 4
- modulus: float32 [2048, 2048], P('dom', 'group'), may hold values from 0.5 to 1.5
- q_weight: float32 [3, 2048, 2048], P(None, 'dom', 'group'), may hold values from 0.005 to 0.05
- adjoint_source: float32 [8, 3, 2048, 2048], P(None, None, 'dom', 'group'), may hold values from -6 to 6
- couple_src: int32 [16, 64, 64, 2], P('group', 'dom'), may hold values from -1 to 31, as said below
- couple_dst: int32 [16, 64, 64, 2], P('group', 'dom'), may hold values from -1 to 31, as said below
- couple_weight: float32 [16, 64, 64, 2], P('group', 'dom'), may hold values from 0.2 to 0.6
Outputs:
- u_end: float32 [3, 2048, 2048], P(None, 'dom', 'group')
- kernel_mu: float32 [2048, 2048], P('dom', 'group')
- kernel_q: float32 [3, 2048, 2048], P(None, 'dom', 'group')
The draws below stay inside these ranges and needn't reach their ends.
Inputs may be any that keep to these rules, and one draw needn't show every extreme that they name: `couple_src`: -1 exactly where the slot is empty; slot s is live only if all slots below s of the same pair are; partition i never couples to itself and always fills all 2 slots towards partition (i + 1) mod 64. couple_dst[c, j, i, s] is -1 exactly where couple_src[c, i, j, s] is.
All inputs are finite; a program needn't handle non-finite values.
Results may differ from the reference program's by a relative error of at most 0.0003.
Values sent between devices are 32-bit elements; how exact they have to be, the bound alone decides.
A program may use at most 32 MiB of HBM per device.

```python
import math
import jax
import jax.numpy as jnp
from jax import lax

CX = 32
CZ = 128
COMP = 3
SLS = 3
STEPS = 8
SLOTS = 2
PARTS_SIZE = 64
GROUPS = 16
NX = 2048
NZ = 2048


def coupling_plan(key):
    key_count, key_src, key_dst = jax.random.split(key, 3)
    count = jax.random.randint(key_count, (GROUPS, PARTS_SIZE, PARTS_SIZE), 0, SLOTS + 1)
    sender = jnp.arange(PARTS_SIZE)[:, None]
    taker = jnp.arange(PARTS_SIZE)[None, :]
    follow = taker == (sender + 1) % PARTS_SIZE
    count = jnp.where(sender == taker, 0, jnp.where(follow, SLOTS, count))
    slot = jnp.arange(SLOTS)
    live = slot[None, None, None, :] < count[..., None]
    src_rows = jax.random.randint(key_src, (GROUPS, PARTS_SIZE, PARTS_SIZE, SLOTS), 0, CX)
    dst_rows = jax.random.randint(key_dst, (GROUPS, PARTS_SIZE, PARTS_SIZE, SLOTS), 0, CX)
    first = follow[None, :, :, None] & (slot[None, None, None, :] == 0)
    src_rows = jnp.where(first, CX - 1, src_rows)
    dst_rows = jnp.where(first, CX - 1, dst_rows)
    src_rows = jnp.where(live, src_rows, -1).astype(jnp.int32)
    dst_rows = jnp.where(live, dst_rows, -1).astype(jnp.int32)
    return (src_rows, dst_rows.transpose(0, 2, 1, 3))


def draw_couple_src(key, part):
    src_rows, dst_rows = coupling_plan(key)
    return src_rows


def draw_couple_dst(key, part):
    src_rows, dst_rows = coupling_plan(key)
    return dst_rows


def levels(key, extent, cuts, low, largest):
    level, own = 1.0, jax.random.fold_in(key, 6)
    for position, shards_of in cuts:
        steps = jnp.exp(jax.random.uniform(jax.random.fold_in(own, position), (shards_of,), jnp.float32, low / len(cuts), largest / len(cuts)))
        level = level * jnp.repeat(steps, extent[position] // shards_of).reshape([-1 if axis == position else 1 for axis in range(len(extent))])
    return level


def centred(own_key, extent, spread, reach, cuts=(), kind=jnp.bfloat16):
    values = spread * jax.random.normal(own_key, extent, jnp.float32)
    if cuts:
        values = values * levels(own_key, extent, cuts, -0.22, 0.18)
    return jnp.clip(values, -reach, reach).astype(kind)


def setup_inputs(seed: int = 0) -> dict:
    keys = jax.random.split(jax.random.key(seed), 10)
    return {
        "u_prev": centred(keys[0], (COMP, NX, NZ), 1.0, 6.0, ((1, 64), (2, 16)), jnp.float32),
        "u_now": centred(keys[1], (COMP, NX, NZ), 1.0, 6.0, ((1, 64), (2, 16)), jnp.float32),
        "memory": centred(keys[2], (SLS, COMP, NX, NZ), 0.3, 4.0, ((2, 64), (3, 16)), jnp.float32),
        "modulus": jnp.clip(0.5 + 1.0 * jax.random.uniform(keys[3], (NX, NZ), jnp.float32) ** levels(keys[3], (NX, NZ), ((0, 64), (1, 16)), -0.2, 0.2), 0.5, 1.5),
        "q_weight": jnp.clip(jnp.exp(math.log(0.05) - 2.3025851 * jax.random.uniform(keys[4], (SLS, NX, NZ), jnp.float32) ** levels(keys[4], (SLS, NX, NZ), ((1, 64), (2, 16)), -0.2, 0.2)), 0.005, 0.05),
        "adjoint_source": centred(keys[5], (STEPS, COMP, NX, NZ), 1.0, 6.0, ((2, 64), (3, 16)), jnp.float32),
        "couple_src": draw_couple_src(jax.random.fold_in(keys[9], 71), 0),
        "couple_dst": draw_couple_dst(jax.random.fold_in(keys[9], 71), 0),
        "couple_weight": jnp.clip(0.2 + 0.400000021 * jax.random.uniform(keys[8], (GROUPS, PARTS_SIZE, PARTS_SIZE, SLOTS), jnp.float32) ** levels(keys[8], (GROUPS, PARTS_SIZE, PARTS_SIZE, SLOTS), ((0, 16), (1, 64)), -0.2, 0.2), 0.2, 0.6),
    }


RELAX = (0.6, 0.85, 0.97)
STEP_SQ = 0.25


def laplace(field):
    padded = jnp.pad(field, ((0, 0), (1, 1), (1, 1)))
    return padded[:, 2:, 1:-1] + padded[:, :-2, 1:-1] + padded[:, 1:-1, 2:] + padded[:, 1:-1, :-2] - 4.0 * field


def couple(radial, couple_src, couple_dst, couple_weight, reverse_flag):
    blocks = radial.reshape(PARTS_SIZE, CX, GROUPS, CZ).transpose(2, 0, 1, 3)
    sender = jnp.broadcast_to(jnp.arange(PARTS_SIZE, dtype=jnp.int32)[:, None, None], (PARTS_SIZE, PARTS_SIZE, SLOTS))
    taker = jnp.broadcast_to(jnp.arange(PARTS_SIZE, dtype=jnp.int32)[None, :, None], (PARTS_SIZE, PARTS_SIZE, SLOTS))

    def one_group(item):
        plane, src_rows, dst_rows, weights = item
        dst_sent = dst_rows.transpose(1, 0, 2)
        live = src_rows >= 0
        factor = jnp.where(live, weights.transpose(1, 0, 2), jnp.float32(0.0))
        src_safe = jnp.maximum(src_rows, 0).astype(jnp.int32)
        dst_safe = jnp.maximum(dst_sent, 0).astype(jnp.int32)
        if reverse_flag:
            values = plane[taker, dst_safe] * factor[..., None]
            return jnp.zeros_like(plane).at[sender, src_safe].add(values)
        values = plane[sender, src_safe] * factor[..., None]
        return jnp.zeros_like(plane).at[taker, dst_safe].add(values)

    result = lax.map(one_group, (blocks, couple_src, couple_dst, couple_weight))
    return result.transpose(1, 2, 0, 3).reshape(NX, NZ)


def reference(u_prev, u_now, memory, modulus, q_weight, adjoint_source, couple_src, couple_dst, couple_weight):
    laps = []
    mems = []
    old, cur, mem = u_prev, u_now, memory
    for step in range(STEPS):
        lap_now = laplace(cur)
        force = modulus * lap_now
        accel = force - jnp.sum(mem, axis=0)
        accel = accel.at[0].add(couple(cur[0], couple_src, couple_dst, couple_weight, False))
        laps.append(lap_now)
        mems.append(mem)
        fresh = 2.0 * cur - old + STEP_SQ * accel
        mem = jnp.stack([RELAX[l] * mem[l] + q_weight[l] * force for l in range(SLS)])
        old, cur = cur, fresh
    v_old = jnp.zeros_like(u_now)
    v_cur = jnp.zeros_like(u_now)
    adj_mem = jnp.zeros_like(memory)
    kernel_mu = jnp.zeros_like(modulus)
    kernel_q = jnp.zeros_like(q_weight)
    for step in reversed(range(STEPS)):
        force = modulus * laplace(v_cur)
        accel = force - jnp.sum(adj_mem, axis=0) + adjoint_source[step]
        accel = accel.at[0].add(couple(v_cur[0], couple_src, couple_dst, couple_weight, True))
        fresh = 2.0 * v_cur - v_old + STEP_SQ * accel
        adj_mem = jnp.stack([RELAX[l] * adj_mem[l] + q_weight[l] * force for l in range(SLS)])
        v_old, v_cur = v_cur, fresh
        kernel_mu = kernel_mu + jnp.sum(v_cur * laps[step], axis=0)
        kernel_q = kernel_q + jnp.sum(v_cur[None] * mems[step], axis=1)
    scale = 1.0 / (3.0 * STEPS)
    return cur, kernel_mu * scale, kernel_q * scale
```

```python
import functools

import jax
import jax.numpy as jnp
from jax import lax
from jax.experimental import pallas as pl
from jax.experimental.pallas import tpu as pltpu
from jax.sharding import PartitionSpec as P

MESH = pl.DeviceIdType.MESH
F32 = jnp.float32
SLS = 3
STEPS = 8
RELAX = (0.6, 0.85, 0.97)
STEP_SQ = 0.25
RUN = 4
HALF = 8
EDGE = 8
SENT = 28
NOW, PREV, MEM, MOD, QW, ADJ = 0, 2, 4, 10, 11, 14


def snake(g, d):
    row, col = lax.div(d, RUN), lax.rem(d, RUN)
    flip = lax.rem(row + (g < HALF).astype(jnp.int32), 2) == 1
    return row * RUN + jnp.where(flip, RUN - 1 - col, col)


def kernel(
    groups,
    parts,
    up_h,
    un_h,
    mem_h,
    mod_h,
    q_h,
    adj_h,
    src_h,
    dst_h,
    wgt_h,
    o_u,
    o_mu,
    o_q,
    i0,
    isrc,
    idst,
    iwgt,
    flip,
    s_1,
    r_1,
    s_2,
    r_2,
    s_b,
    r_b,
    s_o,
    r_o,
    s_e,
    r_e,
    src,
    dst,
    wgt,
    mod0,
    q0,
    adj0,
    xp,
    vp,
    xold,
    vold,
    m0,
    p0,
    cx,
    cv,
    lap0,
    vel0,
    mem0,
    s_l,
    s_r,
    f_l,
    f_r,
    ext,
    zp,
    zold,
    p1,
    lap1,
    vel1,
    mem1,
    s_col,
    r_col,
    in_sem,
    bulk_send,
    bulk_recv,
    side_send,
    side_recv,
    col_send,
    col_recv,
    row_send,
    row_recv,
):
    g, d = lax.axis_index("group"), lax.axis_index("dom")
    last = parts - 1
    turned = lax.rem(g, 2) == 1

    def turn_pos(n):
        return jnp.where(turned, last - n, n)

    place = snake(g, d)
    pos = turn_pos(place)
    has_lo, has_hi = g > 0, g < groups - 1
    at_top, at_end = d > 0, d < last
    first, final = pos == 0, pos == last
    at_left = jnp.logical_or(jnp.logical_not(first), has_lo)
    at_right = jnp.logical_or(jnp.logical_not(final), has_hi)
    prev = snake(g, jnp.maximum(place - 1, 0))
    after = snake(g, jnp.minimum(place + 1, last))
    lo_g, hi_g = jnp.maximum(g - 1, 0), jnp.minimum(g + 1, groups - 1)
    left = (
        jnp.where(first, lo_g, g),
        jnp.where(first, snake(lo_g, place), jnp.where(turned, after, prev)),
    )
    right = (
        jnp.where(final, hi_g, g),
        jnp.where(final, snake(hi_g, place), jnp.where(turned, prev, after)),
    )
    over_lo = jnp.logical_and(first, g == HALF)
    over_hi = jnp.logical_and(jnp.logical_and(final, has_hi), g == HALF - 1)

    def far(t):
        half = lax.div(t + 1, 2)
        step = jnp.where(lax.rem(t, 2) == 1, half, -half)
        return lax.rem(d + parts // 2 + step, parts)

    barrier = pltpu.get_barrier_semaphore()

    def hello(group, part):
        pl.semaphore_signal(barrier, inc=1, device_id=(group, part), device_id_type=MESH)

    def greet(t, carry):
        hello(g, far(t))
        return carry

    beside = []
    for away, group_there in ((-1, has_lo), (1, has_hi)):
        for step, part_there in ((-1, at_top), (0, True), (1, at_end)):
            there = group_there if part_there is True else jnp.logical_and(group_there, part_there)
            beside.append((away, step, there))
    guests = last + over_lo.astype(jnp.int32) + over_hi.astype(jnp.int32)
    for away, step, there in beside:
        pl.when(there)(functools.partial(hello, g + away, d + step))
        guests = guests + there.astype(jnp.int32)
    pl.when(over_lo)(functools.partial(hello, *left))
    pl.when(over_hi)(functools.partial(hello, *right))
    lax.fori_loop(0, last, greet, 0)

    core = pl.ds(EDGE, 32)
    pairs = [
        (un_h.at[0], i0.at[0]),
        (adj_h.at[:, 0], i0.at[pl.ds(5, STEPS)]),
        (src_h, isrc),
        (dst_h, idst),
        (wgt_h, iwgt),
        (up_h.at[0], i0.at[1]),
        (mem_h.at[:, 0], i0.at[pl.ds(2, SLS)]),
        (mod_h, ext.at[0, MOD, core]),
        (q_h, ext.at[0, pl.ds(QW, SLS), core]),
        (un_h.at[pl.ds(1, 2)], ext.at[0, pl.ds(NOW, 2), core]),
        (up_h.at[pl.ds(1, 2)], ext.at[0, pl.ds(PREV, 2), core]),
    ]
    for l in range(SLS):
        pairs.append((mem_h.at[l, pl.ds(1, 2)], ext.at[0, pl.ds(MEM + 2 * l, 2), core]))
    for n in range(STEPS):
        spot = ADJ + 2 * (STEPS - 1 - n)
        pairs.append((adj_h.at[n, pl.ds(1, 2)], ext.at[0, pl.ds(spot, 2), core]))
    loads = []
    for at, (source, target) in enumerate(pairs):
        loads.append(pltpu.make_async_copy(source, target, in_sem.at[at]))
        loads[-1].start()

    def clear(ref, *at):
        def run():
            ref[at] = jnp.zeros_like(ref[at])

        return run

    no = jnp.logical_not
    pl.when(no(at_left))(clear(f_l, slice(None)))
    pl.when(no(at_right))(clear(f_r, slice(None)))
    pl.when(no(at_top))(clear(ext, 0, slice(0, SENT), slice(0, EDGE)))
    pl.when(no(at_end))(clear(ext, 0, slice(0, SENT), slice(EDGE + 32, 2 * EDGE + 32)))
    for away, step, there in beside:
        pl.when(no(there))(clear(r_col, (away + 1) // 2, step + 1))
    zp[...] = jnp.zeros_like(zp)
    zold[...] = jnp.zeros_like(zold)
    p1[...] = jnp.zeros_like(p1)

    lane = lax.broadcasted_iota(jnp.int32, (32, 128), 1)
    low = lane < 64
    edge = lax.broadcasted_iota(jnp.int32, (128, 128), 1)
    wide = edge < 64
    zero = jnp.zeros((32, 128), F32)

    for load in loads:
        load.wait()

    def pack4(planes, target, row):
        flip[...] = jnp.concatenate(planes, axis=0).T
        target[pl.ds(row, parts, stride=8), :] = flip[pl.ds(0, parts, stride=2), :]
        target[pl.ds(row + 1, parts, stride=8), :] = flip[pl.ds(1, parts, stride=2), :]

    flip[...] = jnp.concatenate([i0[0], i0[5 + STEPS - 1], zero, zero], axis=0).T
    s_1[pl.ds(0, parts, stride=8), :] = jnp.where(
        wide[0:64],
        flip[pl.ds(0, parts, stride=2), :],
        pltpu.roll(flip[pl.ds(1, parts, stride=2), :], 64, 1),
    )
    for t, table in enumerate((isrc, idst, iwgt)):
        row = jnp.concatenate([table[0:1, :].astype(F32), table[1:2, :].astype(F32)], axis=1)
        s_2[pl.ds(t, parts, stride=8), :] = jnp.broadcast_to(row, (parts, 128))
    pack4([i0[1], i0[2], i0[3], i0[4]], s_2, 3)
    pack4([ext[0, MOD, core], ext[0, QW, core], ext[0, QW + 1, core], ext[0, QW + 2, core]], s_2, 5)
    pack4([i0[5], i0[6], i0[7], i0[8]], s_b, 0)
    pack4([i0[9], i0[10], i0[11], i0[11]], s_b, 2)

    for t in range(SENT // 4):
        tile = ext[0, 4 * t : 4 * t + 4, core, :].reshape(128, 128).T
        s_col[0, t] = tile[0:EDGE]
        s_col[1, t] = tile[128 - EDGE :]

    pl.semaphore_wait(barrier, guests)

    def spread(source, target, rows, which, by_pos):
        def send(t, carry):
            peer = far(t)
            take = turn_pos(snake(g, peer)) if by_pos else peer
            land = d if by_pos else pos
            pltpu.make_async_remote_copy(
                src_ref=source.at[pl.ds(pl.multiple_of(take * 8, 8), rows), :],
                dst_ref=target.at[pl.ds(pl.multiple_of(land * 8, 8), rows), :],
                send_sem=bulk_send.at[which],
                recv_sem=bulk_recv.at[which],
                device_id=(g, peer),
                device_id_type=MESH,
            ).start()
            return carry

        lax.fori_loop(0, last, send, 0)
        mine = pl.ds(pl.multiple_of((pos if by_pos else d) * 8, 8), 8)
        here = pl.ds(pl.multiple_of((d if by_pos else pos) * 8, 8), 8)
        target[here, :] = source[mine, :]

    def bulk(source, target, rows, which):
        return pltpu.make_async_remote_copy(
            src_ref=source.at[pl.ds(0, last * rows), :],
            dst_ref=target.at[pl.ds(0, last * rows), :],
            send_sem=bulk_send.at[which],
            recv_sem=bulk_recv.at[which],
            device_id=(g, lax.rem(d + 1, parts)),
            device_id_type=MESH,
        )

    def start_all(copies):
        for cond, copy, _ in copies:
            pl.when(cond)(copy.start)

    def recv_all(copies):
        for _, copy, cond in copies:
            pl.when(cond)(copy.wait_recv)

    def sent_all(copies):
        for cond, copy, _ in copies:
            pl.when(cond)(copy.wait_send)

    halo1 = []
    for at, (away, step, there) in enumerate(beside):
        side, back = (away + 1) // 2, len(beside) - 1 - at
        halo1.append(
            (
                there,
                pltpu.make_async_remote_copy(
                    src_ref=s_col.at[side],
                    dst_ref=r_col.at[1 - side, 1 - step],
                    send_sem=col_send.at[at],
                    recv_sem=col_recv.at[back],
                    device_id=(g + away, d + step),
                    device_id_type=MESH,
                ),
                beside[back][2],
            )
        )
    planes = pl.ds(0, SENT)
    for at, (step, there, source, target, other) in enumerate(
        ((-1, at_top, EDGE, EDGE + 32, at_end), (1, at_end, 32, 0, at_top))
    ):
        halo1.append(
            (
                there,
                pltpu.make_async_remote_copy(
                    src_ref=ext.at[0, planes, pl.ds(source, EDGE)],
                    dst_ref=ext.at[0, planes, pl.ds(target, EDGE)],
                    send_sem=row_send.at[at],
                    recv_sem=row_recv.at[at],
                    device_id=(g, d + step),
                    device_id_type=MESH,
                ),
                other,
            )
        )

    spread(s_1, r_1, 1, 0, True)
    start_all(halo1)
    spread(s_2, r_2, 7, 1, True)
    spread(s_b, r_b, 4, 2, True)

    def unpack(source, first, second):
        return jnp.concatenate(
            [
                source[pl.ds(first, parts, stride=8), :],
                source[pl.ds(second, parts, stride=8), :],
            ],
            axis=0,
        ).T

    def halo0(slot):
        return (
            (
                at_left,
                pltpu.make_async_remote_copy(
                    src_ref=s_l.at[slot],
                    dst_ref=f_r.at[slot],
                    send_sem=side_send.at[slot, 0],
                    recv_sem=side_recv.at[slot, 1],
                    device_id=left,
                    device_id_type=MESH,
                ),
                at_right,
            ),
            (
                at_right,
                pltpu.make_async_remote_copy(
                    src_ref=s_r.at[slot],
                    dst_ref=f_l.at[slot],
                    send_sem=side_send.at[slot, 1],
                    recv_sem=side_recv.at[slot, 0],
                    device_id=right,
                    device_id_type=MESH,
                ),
                at_left,
            ),
        )

    def show(slot, x, v):
        s_l[slot] = jnp.where(low, x, pltpu.roll(v, 64, 1))
        s_r[slot] = jnp.where(low, pltpu.roll(x, 64, 1), v)
        start_all(halo0(slot))

    bulk(s_1, r_1, 1, 0).wait_recv()
    both = unpack(r_1, 0, 0)
    x = jnp.where(low, both[0:32], both[64:96])
    v = STEP_SQ * jnp.where(low, both[32:64], both[96:128])
    show(0, x, v)
    xp[8:40, :] = x
    vp[8:40, :] = v
    vel0[STEPS - 1] = v
    vold[...] = zero
    for l in range(SLS):
        p0[l] = zero

    recv_all(halo1)
    inner = lax.rem(lax.broadcasted_iota(jnp.int32, (EDGE, 128), 1), 32) < 16
    blank = jnp.zeros((128 - 2 * EDGE, 128), F32)

    def beside_planes(tiles):
        return jnp.concatenate([tiles[1], blank, tiles[0]], axis=0).T.reshape(4, 32, 128)

    for t in range(SENT // 4):
        four = slice(4 * t, 4 * t + 4)
        ext[1, four, core, :] = beside_planes([r_col[side, 1, t] for side in range(2)])
        ends = beside_planes(
            [jnp.where(inner, r_col[side, 2, t], r_col[side, 0, t]) for side in range(2)]
        )
        ext[1, four, 0:EDGE, :] = ends[:, 32 - EDGE :, :]
        ext[1, four, EDGE + 32 : 2 * EDGE + 32, :] = ends[:, 0:EDGE, :]
    sent_all(halo1)
    for c in range(2):
        for t in range(2):
            zp[c, t, 8:56, :] = ext[t, NOW + c]
            zp[c + 2, t, 8:56, :] = STEP_SQ * ext[t, ADJ + c]
            zold[c, t] = ext[t, PREV + c]
        vel1[STEPS, c] = STEP_SQ * ext[0, ADJ + c, core, :]

    rim = lax.broadcasted_iota(jnp.int32, (48, 128), 1)

    def around(f):
        main, side = zp[f, 0, 8:56, :], zp[f, 1, 8:56, :]
        lap = []
        ahead = [pltpu.roll(a, 127, 1) for a in (main, side)]
        behind = [pltpu.roll(a, 1, 1) for a in (main, side)]
        for t, centre in enumerate((main, side)):
            lap.append(
                zp[f, t, 9:57, :]
                + zp[f, t, 7:55, :]
                + jnp.where(rim == 127, ahead[1 - t], ahead[t])
                + jnp.where(rim == 0, behind[1 - t], behind[t])
                - 4.0 * centre
            )
        return (main, side), lap

    def round1(k, carry):
        n = STEPS - 2 - k
        source = ADJ + 2 * jnp.minimum(k + 1, STEPS - 1)
        for c in range(2):
            now, lap = around(c)
            lap1[k, c] = lap[0][8:40]
            for l in range(SLS):
                mem1[k, l, c] = ext[0, MEM + 2 * l + c, core, :]
            for t in range(2):
                kept = [ext[t, MEM + 2 * l + c] for l in range(SLS)]
                force = ext[t, MOD] * lap[t]
                accel = force - (kept[0] + kept[1] + kept[2])
                fresh = 2.0 * now[t] - zold[c, t] + STEP_SQ * accel
                for l in range(SLS):
                    ext[t, MEM + 2 * l + c] = RELAX[l] * kept[l] + ext[t, QW + l] * force
                zold[c, t] = now[t]
                zp[c, t, 8:56, :] = fresh
            now, lap = around(c + 2)
            for t in range(2):
                kept = [p1[l, c, t] for l in range(SLS)]
                force = ext[t, MOD] * lap[t]
                accel = force - (kept[0] + kept[1] + kept[2]) + ext[t, source + c]
                fresh = 2.0 * now[t] - zold[c + 2, t] + STEP_SQ * accel
                for l in range(SLS):
                    p1[l, c, t] = RELAX[l] * kept[l] + ext[t, QW + l] * force
                zold[c + 2, t] = now[t]
                zp[c + 2, t, 8:56, :] = fresh
                if t == 0:
                    vel1[n + 1, c] = fresh[8:40]
        return carry

    lax.fori_loop(0, STEPS, round1, 0)

    def terms(vel, lap, mem, count):
        mu = zero
        q = [zero] * SLS
        for n in range(count):
            mu = mu + vel(n) * lap(n)
            for l in range(SLS):
                q[l] = q[l] + vel(n) * mem(n, l)
        return mu, q

    mu_sum, q_sum = zero, [zero] * SLS
    for c in range(2):
        o_u[c + 1] = zp[c, 0, 16:48, :]
        mu, q = terms(
            lambda n: vel1[n + 1, c], lambda n: lap1[n, c], lambda n, l: mem1[n, l, c], STEPS
        )
        mu_sum = mu_sum + mu
        q_sum = [a + b for a, b in zip(q_sum, q)]
    o_mu[...] = mu_sum
    for l in range(SLS):
        o_q[l] = q_sum[l]

    bulk(s_2, r_2, 7, 1).wait_recv()
    four = unpack(r_2, 3, 4)
    xold[...] = four[0:32]
    for l in range(SLS):
        m0[l] = four[32 + 32 * l : 64 + 32 * l]
    four = unpack(r_2, 5, 6)
    mod0[...] = four[0:32]
    for l in range(SLS):
        q0[l] = four[32 + 32 * l : 64 + 32 * l]
    src[...] = unpack(r_2, 0, 0)
    dst[...] = unpack(r_2, 1, 1)
    wgt[...] = unpack(r_2, 2, 2)

    def swap(a):
        t = a.T
        top, bottom = t[0:64], t[64:128]
        half = wide[0:64]
        return jnp.concatenate(
            [
                jnp.where(half, top, pltpu.roll(bottom, 64, 1)),
                jnp.where(half, pltpu.roll(top, 64, 1), bottom),
            ],
            axis=0,
        )

    def pick(table, plane):
        rows = table[...]
        out = jnp.zeros((128, 128), F32)
        for r in range(32):
            out = jnp.where(rows == float(r), plane[8 + r : 9 + r, :], out)
        return out

    def drop(table, values, out):
        rows = table[...]
        for r in range(32):
            out[r : r + 1, :] = jnp.sum(
                jnp.where(rows == float(r), values, 0.0), axis=0, keepdims=True
            )

    part = lax.rem(lax.broadcasted_iota(jnp.int32, (1, 128), 1), 64)

    def rims(plane):
        plane[7:8, :] = jnp.where(part == 0, 0.0, pltpu.roll(plane[39:40, :], 1, 1))
        plane[40:41, :] = jnp.where(part == 63, 0.0, pltpu.roll(plane[8:9, :], 127, 1))

    def ready(now, old, kept, other, turned_now, plane):
        own = plane[9:41, :] + plane[7:39, :] + turned_now - 4.0 * now
        rest = 2.0 * now - old + STEP_SQ * (other - (kept[0] + kept[1] + kept[2]))
        return own, rest

    def round0(k, adjoint):
        slot = lax.rem(k, 2)
        copies = halo0(slot)
        drop(dst, swap(pick(src, xp)) * wgt[...], cx)
        rims(xp)
        x = xp[8:40, :]
        m = [m0[l] for l in range(SLS)]
        x_own, x_rest = ready(x, xold[...], m, cx[...], pltpu.roll(x, 64, 1), xp)
        if adjoint:
            drop(src, swap(pick(dst, vp) * wgt[...]), cv)
            rims(vp)

            @pl.when(k == 0)
            def _():
                bulk(s_b, r_b, 4, 2).wait_recv()
                four = unpack(r_b, 0, 1)
                for n in range(4):
                    adj0[n] = four[n * 32 : n * 32 + 32]
                four = unpack(r_b, 2, 3)
                for n in range(3):
                    adj0[n + 4] = four[n * 32 : n * 32 + 32]

            n = STEPS - 2 - k
            v = vp[8:40, :]
            p = [p0[l] for l in range(SLS)]
            v_own, v_rest = ready(v, vold[...], p, cv[...] + adj0[n], pltpu.roll(v, 64, 1), vp)
        recv_all(copies)
        from_l, from_r = f_l[slot], f_r[slot]
        lap = x_own + jnp.where(low, from_l, pltpu.roll(from_r, 64, 1))
        force = mod0[...] * lap
        fresh = x_rest + STEP_SQ * force
        if adjoint:
            v_force = mod0[...] * (v_own + jnp.where(low, pltpu.roll(from_l, 64, 1), from_r))
            v_fresh = v_rest + STEP_SQ * v_force
            show(1 - slot, fresh, v_fresh)
        lap0[k] = lap
        xold[...] = x
        xp[8:40, :] = fresh
        if adjoint:
            for l in range(SLS):
                mem0[k, l] = m[l]
                m0[l] = RELAX[l] * m[l] + q0[l] * force
                p0[l] = RELAX[l] * p[l] + q0[l] * v_force
            vold[...] = v
            vp[8:40, :] = v_fresh
            vel0[n] = v_fresh
        sent_all(copies)

    def step0(k, carry):
        round0(k, True)
        return carry

    lax.fori_loop(0, STEPS - 1, step0, 0)

    mu, _ = terms(lambda n: vel0[n], lambda n: lap0[n], lambda n, l: zero, STEPS - 1)
    q = [zero] * SLS
    for n in range(STEPS):
        for l in range(SLS):
            q[l] = q[l] + vel0[n] * (mem0[n, l] if n < STEPS - 1 else m0[l])
    turn = jnp.concatenate([mu] + q, axis=0).T
    s_o[pl.ds(0, parts, stride=8), :] = turn[0:64]
    s_o[pl.ds(1, parts, stride=8), :] = turn[64:128]
    spread(s_o, r_o, 2, 3, False)

    round0(STEPS - 1, False)

    turn = jnp.concatenate([xp[8:40, :], vel0[STEPS - 1] * lap0[STEPS - 1], zero, zero], axis=0).T
    s_e[pl.ds(0, parts, stride=8), :] = jnp.where(
        wide[0:64], turn[0:64], pltpu.roll(turn[64:128], 64, 1)
    )
    spread(s_e, r_e, 1, 4, False)

    bulk(s_o, r_o, 2, 3).wait_recv()
    flip[pl.ds(0, parts, stride=2), :] = r_o[pl.ds(0, parts, stride=8), :]
    flip[pl.ds(1, parts, stride=2), :] = r_o[pl.ds(1, parts, stride=8), :]
    four = flip[...].T
    scale = 1.0 / (3.0 * STEPS)
    mu = o_mu[...] + four[0:32]
    for l in range(SLS):
        o_q[l] = (o_q[l] + four[32 + 32 * l : 64 + 32 * l]) * scale
    bulk(s_e, r_e, 1, 4).wait_recv()
    ends = r_e[pl.ds(0, parts, stride=8), :]
    flip[pl.ds(0, parts, stride=2), :] = ends
    flip[pl.ds(1, parts, stride=2), :] = pltpu.roll(ends, 64, 1)
    four = flip[...].T
    o_u[0] = four[0:32]
    o_mu[...] = (mu + four[32:64]) * scale

    bulk(s_1, r_1, 1, 0).wait_send()
    bulk(s_2, r_2, 7, 1).wait_send()
    bulk(s_b, r_b, 4, 2).wait_send()
    bulk(s_o, r_o, 2, 3).wait_send()
    bulk(s_e, r_e, 1, 4).wait_send()


def solution(mesh):
    groups, parts = mesh.shape["group"], mesh.shape["dom"]

    def shards(
        u_prev, u_now, memory, modulus, q_weight, adjoint_source, couple_src, couple_dst, couple_weight
    ):
        tables = [t.reshape(parts, -1).T for t in (couple_src, couple_dst, couple_weight)]
        plane = (32, 128)
        square = (128, 128)

        def vmem(*shape):
            return pltpu.VMEM(shape, F32)

        dma = pltpu.SemaphoreType.DMA
        return pl.pallas_call(
            functools.partial(kernel, groups, parts),
            out_shape=(
                jax.ShapeDtypeStruct(u_now.shape, F32),
                jax.ShapeDtypeStruct(modulus.shape, F32),
                jax.ShapeDtypeStruct(q_weight.shape, F32),
            ),
            in_specs=[pl.BlockSpec(memory_space=pltpu.HBM)] * 9,
            out_specs=[pl.BlockSpec(memory_space=pltpu.VMEM)] * 3,
            scratch_shapes=[
                vmem(5 + STEPS, *plane),
                pltpu.VMEM((2, parts), jnp.int32),
                pltpu.VMEM((2, parts), jnp.int32),
                vmem(2, parts),
                vmem(*square),
            ]
            + [vmem(parts * 8, 128)] * 10
            + [
                vmem(*square),
                vmem(*square),
                vmem(*square),
                vmem(*plane),
                vmem(SLS, *plane),
                vmem(STEPS - 1, *plane),
                vmem(48, 128),
                vmem(48, 128),
                vmem(*plane),
                vmem(*plane),
                vmem(SLS, *plane),
                vmem(SLS, *plane),
                vmem(*plane),
                vmem(*plane),
                vmem(STEPS, *plane),
                vmem(STEPS, *plane),
                vmem(STEPS, SLS, *plane),
                vmem(2, *plane),
                vmem(2, *plane),
                vmem(2, *plane),
                vmem(2, *plane),
                vmem(2, SENT + 2, 48, 128),
                vmem(4, 2, 64, 128),
                vmem(4, 2, 48, 128),
                vmem(SLS, 2, 2, 48, 128),
                vmem(STEPS, 2, *plane),
                vmem(STEPS + 1, 2, *plane),
                vmem(STEPS, SLS, 2, *plane),
                vmem(2, SENT // 4, EDGE, 128),
                vmem(2, 3, SENT // 4, EDGE, 128),
                dma((22,)),
                dma((5,)),
                dma((5,)),
                dma((2, 2)),
                dma((2, 2)),
                dma((6,)),
                dma((6,)),
                dma((2,)),
                dma((2,)),
            ],
            compiler_params=pltpu.CompilerParams(
                collective_id=0, has_side_effects=True, vmem_limit_bytes=60 * 1024 * 1024
            ),
        )(u_prev, u_now, memory, modulus, q_weight, adjoint_source, *tables)

    in_specs = (
        P(None, "dom", "group"),
        P(None, "dom", "group"),
        P(None, None, "dom", "group"),
        P("dom", "group"),
        P(None, "dom", "group"),
        P(None, None, "dom", "group"),
        P("group", "dom", None, None),
        P("group", "dom", None, None),
        P("group", "dom", None, None),
    )
    out_specs = (P(None, "dom", "group"), P("dom", "group"), P(None, "dom", "group"))
    return jax.shard_map(shards, mesh=mesh, in_specs=in_specs, out_specs=out_specs, check_vma=False)
```

```python
import functools

import jax
import jax.numpy as jnp
from jax import lax
from jax.experimental import pallas as pl
from jax.experimental.pallas import tpu as pltpu
from jax.sharding import PartitionSpec as P

MESH = pl.DeviceIdType.MESH
F32 = jnp.float32
SLS = 3
STEPS = 8
RELAX = (0.6, 0.85, 0.97)
STEP_SQ = 0.25
RUN = 4
HALF = 8
EDGE = 8
SENT = 28
NOW, PREV, MEM, MOD, QW, ADJ = 0, 2, 4, 10, 11, 14


def snake(g, d):
    row, col = lax.div(d, RUN), lax.rem(d, RUN)
    flip = lax.rem(row + (g < HALF).astype(jnp.int32), 2) == 1
    return row * RUN + jnp.where(flip, RUN - 1 - col, col)


def kernel(
    groups,
    parts,
    up_h,
    un_h,
    mem_h,
    mod_h,
    q_h,
    adj_h,
    src_h,
    dst_h,
    wgt_h,
    o_u,
    o_mu,
    o_q,
    i0,
    isrc,
    idst,
    iwgt,
    flip,
    s_1,
    r_1,
    s_2,
    r_2,
    s_b,
    r_b,
    s_t,
    r_t,
    flat,
    s_o,
    r_o,
    s_e,
    r_e,
    src,
    dst,
    wgt,
    mod0,
    q0,
    adj0,
    xp,
    vp,
    xold,
    vold,
    m0,
    p0,
    cx,
    cv,
    lap0,
    vel0,
    mem0,
    s_l,
    s_r,
    f_l,
    f_r,
    ext,
    zp,
    zold,
    p1,
    lap1,
    vel1,
    mem1,
    s_col,
    r_col,
    in_sem,
    bulk_send,
    bulk_recv,
    side_send,
    side_recv,
    col_send,
    col_recv,
    row_send,
    row_recv,
    tab_send,
    tab_recv,
):
    g, d = lax.axis_index("group"), lax.axis_index("dom")
    last = parts - 1
    turned = lax.rem(g, 2) == 1

    def turn_pos(n):
        return jnp.where(turned, last - n, n)

    place = snake(g, d)
    pos = turn_pos(place)
    has_lo, has_hi = g > 0, g < groups - 1
    at_top, at_end = d > 0, d < last
    first, final = pos == 0, pos == last
    at_left = jnp.logical_or(jnp.logical_not(first), has_lo)
    at_right = jnp.logical_or(jnp.logical_not(final), has_hi)
    prev = snake(g, jnp.maximum(place - 1, 0))
    after = snake(g, jnp.minimum(place + 1, last))
    lo_g, hi_g = jnp.maximum(g - 1, 0), jnp.minimum(g + 1, groups - 1)
    left = (
        jnp.where(first, lo_g, g),
        jnp.where(first, snake(lo_g, place), jnp.where(turned, after, prev)),
    )
    right = (
        jnp.where(final, hi_g, g),
        jnp.where(final, snake(hi_g, place), jnp.where(turned, prev, after)),
    )
    over_lo = jnp.logical_and(first, g == HALF)
    over_hi = jnp.logical_and(jnp.logical_and(final, has_hi), g == HALF - 1)

    def far(t):
        half = lax.div(t + 1, 2)
        step = jnp.where(lax.rem(t, 2) == 1, half, -half)
        return lax.rem(d + parts // 2 + step, parts)

    barrier = pltpu.get_barrier_semaphore()

    def hello(group, part):
        pl.semaphore_signal(barrier, inc=1, device_id=(group, part), device_id_type=MESH)

    def greet(t, carry):
        hello(g, far(t))
        return carry

    beside = []
    for away, group_there in ((-1, has_lo), (1, has_hi)):
        for step, part_there in ((-1, at_top), (0, True), (1, at_end)):
            there = group_there if part_there is True else jnp.logical_and(group_there, part_there)
            beside.append((away, step, there))
    guests = last + over_lo.astype(jnp.int32) + over_hi.astype(jnp.int32)
    for away, step, there in beside:
        pl.when(there)(functools.partial(hello, g + away, d + step))
        guests = guests + there.astype(jnp.int32)
    pl.when(over_lo)(functools.partial(hello, *left))
    pl.when(over_hi)(functools.partial(hello, *right))
    lax.fori_loop(0, last, greet, 0)

    core = pl.ds(EDGE, 32)
    pairs = [
        (un_h.at[0], i0.at[0]),
        (adj_h.at[:, 0], i0.at[pl.ds(5, STEPS)]),
        (src_h, isrc),
        (dst_h, idst),
        (wgt_h, iwgt),
        (up_h.at[0], i0.at[1]),
        (mem_h.at[:, 0], i0.at[pl.ds(2, SLS)]),
        (mod_h, ext.at[0, MOD, core]),
        (q_h, ext.at[0, pl.ds(QW, SLS), core]),
        (un_h.at[pl.ds(1, 2)], ext.at[0, pl.ds(NOW, 2), core]),
        (up_h.at[pl.ds(1, 2)], ext.at[0, pl.ds(PREV, 2), core]),
    ]
    for l in range(SLS):
        pairs.append((mem_h.at[l, pl.ds(1, 2)], ext.at[0, pl.ds(MEM + 2 * l, 2), core]))
    for n in range(STEPS):
        spot = ADJ + 2 * (STEPS - 1 - n)
        pairs.append((adj_h.at[n, pl.ds(1, 2)], ext.at[0, pl.ds(spot, 2), core]))
    loads = []
    for at, (source, target) in enumerate(pairs):
        loads.append(pltpu.make_async_copy(source, target, in_sem.at[at]))
        loads[-1].start()

    def clear(ref, *at):
        def run():
            ref[at] = jnp.zeros_like(ref[at])

        return run

    no = jnp.logical_not
    pl.when(no(at_left))(clear(f_l, slice(None)))
    pl.when(no(at_right))(clear(f_r, slice(None)))
    pl.when(no(at_top))(clear(ext, 0, slice(0, SENT), slice(0, EDGE)))
    pl.when(no(at_end))(clear(ext, 0, slice(0, SENT), slice(EDGE + 32, 2 * EDGE + 32)))
    for away, step, there in beside:
        pl.when(no(there))(clear(r_col, (away + 1) // 2, step + 1))
    zp[...] = jnp.zeros_like(zp)
    zold[...] = jnp.zeros_like(zold)
    p1[...] = jnp.zeros_like(p1)

    lane = lax.broadcasted_iota(jnp.int32, (32, 128), 1)
    low = lane < 64
    edge = lax.broadcasted_iota(jnp.int32, (128, 128), 1)
    wide = edge < 64
    zero = jnp.zeros((32, 128), F32)

    for load in loads:
        load.wait()

    def pack4(planes, target, row):
        flip[...] = jnp.concatenate(planes, axis=0).T
        target[pl.ds(row, parts, stride=8), :] = flip[pl.ds(0, parts, stride=2), :]
        target[pl.ds(row + 1, parts, stride=8), :] = flip[pl.ds(1, parts, stride=2), :]

    def pack2(planes, target, row):
        flip[...] = jnp.concatenate(planes + [zero, zero], axis=0).T
        target[pl.ds(row, parts, stride=8), :] = jnp.where(
            wide[0:64],
            flip[pl.ds(0, parts, stride=2), :],
            pltpu.roll(flip[pl.ds(1, parts, stride=2), :], 64, 1),
        )

    adj = 5
    pack2([i0[0], i0[adj + 7]], s_1, 0)
    for t, table in enumerate((isrc, idst, iwgt)):
        row = jnp.concatenate([table[0:1, :].astype(F32), table[1:2, :].astype(F32)], axis=1)
        s_t[t : t + 1, :] = row
    pack4([i0[1], i0[2], i0[3], i0[4]], s_2, 0)
    pack4([ext[0, MOD, core], ext[0, QW, core], ext[0, QW + 1, core], ext[0, QW + 2, core]], s_2, 2)
    pack2([i0[adj + 6], i0[adj + 5]], s_2, 4)
    pack4([i0[adj + 4], i0[adj + 3], i0[adj + 2], i0[adj + 1]], s_b, 0)
    pack2([i0[adj], zero], s_b, 2)

    for t in range(SENT // 4):
        tile = ext[0, 4 * t : 4 * t + 4, core, :].reshape(128, 128).T
        s_col[0, t] = tile[0:EDGE]
        s_col[1, t] = tile[128 - EDGE :]

    pl.semaphore_wait(barrier, guests)

    def spread(source, target, rows, which, by_pos):
        def send(t, carry):
            peer = far(t)
            take = turn_pos(snake(g, peer)) if by_pos else peer
            land = d if by_pos else pos
            pltpu.make_async_remote_copy(
                src_ref=source.at[pl.ds(pl.multiple_of(take * 8, 8), rows), :],
                dst_ref=target.at[pl.ds(pl.multiple_of(land * 8, 8), rows), :],
                send_sem=bulk_send.at[which],
                recv_sem=bulk_recv.at[which],
                device_id=(g, peer),
                device_id_type=MESH,
            ).start()
            return carry

        lax.fori_loop(0, last, send, 0)
        mine = pl.ds(pl.multiple_of((pos if by_pos else d) * 8, 8), 8)
        here = pl.ds(pl.multiple_of((d if by_pos else pos) * 8, 8), 8)
        target[here, :] = source[mine, :]

    def bulk(source, target, rows, which):
        return pltpu.make_async_remote_copy(
            src_ref=source.at[pl.ds(0, last * rows), :],
            dst_ref=target.at[pl.ds(0, last * rows), :],
            send_sem=bulk_send.at[which],
            recv_sem=bulk_recv.at[which],
            device_id=(g, lax.rem(d + 1, parts)),
            device_id_type=MESH,
        )

    def start_all(copies):
        for cond, copy, _ in copies:
            pl.when(cond)(copy.start)

    def recv_all(copies):
        for _, copy, cond in copies:
            pl.when(cond)(copy.wait_recv)

    def sent_all(copies):
        for cond, copy, _ in copies:
            pl.when(cond)(copy.wait_send)

    halo1 = []
    for at, (away, step, there) in enumerate(beside):
        side, back = (away + 1) // 2, len(beside) - 1 - at
        halo1.append(
            (
                there,
                pltpu.make_async_remote_copy(
                    src_ref=s_col.at[side],
                    dst_ref=r_col.at[1 - side, 1 - step],
                    send_sem=col_send.at[at],
                    recv_sem=col_recv.at[back],
                    device_id=(g + away, d + step),
                    device_id_type=MESH,
                ),
                beside[back][2],
            )
        )
    planes = pl.ds(0, SENT)
    for at, (step, there, source, target, other) in enumerate(
        ((-1, at_top, EDGE, EDGE + 32, at_end), (1, at_end, 32, 0, at_top))
    ):
        halo1.append(
            (
                there,
                pltpu.make_async_remote_copy(
                    src_ref=ext.at[0, planes, pl.ds(source, EDGE)],
                    dst_ref=ext.at[0, planes, pl.ds(target, EDGE)],
                    send_sem=row_send.at[at],
                    recv_sem=row_recv.at[at],
                    device_id=(g, d + step),
                    device_id_type=MESH,
                ),
                other,
            )
        )

    lines, depth = parts // RUN, 3
    line, spot = lax.div(d, RUN), lax.rem(d, RUN)
    slab = pl.ds(pl.multiple_of(spot * 8, 8), depth)

    def along(t, carry):
        half = lax.div(t + 1, 2)
        step = jnp.where(lax.rem(t, 2) == 1, half, -half)
        peer = lax.rem(line + lines // 2 + step, lines)
        pltpu.make_async_remote_copy(
            src_ref=s_t.at[pl.ds(0, depth)],
            dst_ref=r_t.at[line, slab],
            send_sem=tab_send.at[0],
            recv_sem=tab_recv.at[0],
            device_id=(g, peer * RUN + spot),
            device_id_type=MESH,
        ).start()
        return carry

    across = [
        pltpu.make_async_remote_copy(
            src_ref=r_t.at[:, slab],
            dst_ref=r_t.at[:, slab],
            send_sem=tab_send.at[step],
            recv_sem=tab_recv.at[step],
            device_id=(g, line * RUN + lax.rem(spot + step, RUN)),
            device_id_type=MESH,
        )
        for step in range(1, RUN)
    ]
    tables = pltpu.make_async_remote_copy(
        src_ref=r_t.at[pl.ds(0, lines - 1), pl.ds(0, depth)],
        dst_ref=r_t.at[pl.ds(0, lines - 1), pl.ds(0, depth)],
        send_sem=tab_send.at[0],
        recv_sem=tab_recv.at[0],
        device_id=(g, lax.rem(d + 1, parts)),
        device_id_type=MESH,
    )

    lax.fori_loop(0, lines - 1, along, 0)
    r_t[line, slab, :] = s_t[0:depth, :]
    spread(s_1, r_1, 1, 0, True)
    spread(s_2, r_2, 5, 1, True)
    spread(s_b, r_b, 3, 2, True)

    def unpack(source, first, second):
        return jnp.concatenate(
            [
                source[pl.ds(first, parts, stride=8), :],
                source[pl.ds(second, parts, stride=8), :],
            ],
            axis=0,
        ).T

    def halo0(slot):
        return (
            (
                at_left,
                pltpu.make_async_remote_copy(
                    src_ref=s_l.at[slot],
                    dst_ref=f_r.at[slot],
                    send_sem=side_send.at[slot, 0],
                    recv_sem=side_recv.at[slot, 1],
                    device_id=left,
                    device_id_type=MESH,
                ),
                at_right,
            ),
            (
                at_right,
                pltpu.make_async_remote_copy(
                    src_ref=s_r.at[slot],
                    dst_ref=f_l.at[slot],
                    send_sem=side_send.at[slot, 1],
                    recv_sem=side_recv.at[slot, 0],
                    device_id=right,
                    device_id_type=MESH,
                ),
                at_left,
            ),
        )

    def show(slot, x, v):
        s_l[slot] = jnp.where(low, x, pltpu.roll(v, 64, 1))
        s_r[slot] = jnp.where(low, pltpu.roll(x, 64, 1), v)
        start_all(halo0(slot))

    def unpack2(source, row):
        both = unpack(source, row, row)
        return [jnp.where(low, both[at : at + 32], both[at + 64 : at + 96]) for at in (0, 32)]

    tables.wait_recv()
    for copy in across:
        copy.start()
    bulk(s_1, r_1, 1, 0).wait_recv()
    x, v = unpack2(r_1, 0)
    v = STEP_SQ * v
    show(0, x, v)
    xp[8:40, :] = x
    vp[8:40, :] = v
    vel0[STEPS - 1] = v
    vold[...] = zero
    for l in range(SLS):
        p0[l] = zero

    for copy in across:
        copy.wait()
    flat[...] = r_t[...].reshape(parts * 8, 128)
    src[...] = unpack(flat, 0, 0)
    dst[...] = unpack(flat, 1, 1)
    wgt[...] = unpack(flat, 2, 2)
    bulk(s_2, r_2, 5, 1).wait_recv()
    four = unpack(r_2, 0, 1)
    xold[...] = four[0:32]
    for l in range(SLS):
        m0[l] = four[32 + 32 * l : 64 + 32 * l]
    four = unpack(r_2, 2, 3)
    mod0[...] = four[0:32]
    for l in range(SLS):
        q0[l] = four[32 + 32 * l : 64 + 32 * l]
    adj0[6], adj0[5] = unpack2(r_2, 4)

    def swap(a):
        t = a.T
        top, bottom = t[0:64], t[64:128]
        half = wide[0:64]
        return jnp.concatenate(
            [
                jnp.where(half, top, pltpu.roll(bottom, 64, 1)),
                jnp.where(half, pltpu.roll(top, 64, 1), bottom),
            ],
            axis=0,
        )

    def pick(table, plane):
        rows = table[...]
        out = jnp.zeros((128, 128), F32)
        for r in range(32):
            out = jnp.where(rows == float(r), plane[8 + r : 9 + r, :], out)
        return out

    def drop(table, values, out):
        rows = table[...]
        for r in range(32):
            out[r : r + 1, :] = jnp.sum(
                jnp.where(rows == float(r), values, 0.0), axis=0, keepdims=True
            )

    part = lax.rem(lax.broadcasted_iota(jnp.int32, (1, 128), 1), 64)

    def rims(plane):
        plane[7:8, :] = jnp.where(part == 0, 0.0, pltpu.roll(plane[39:40, :], 1, 1))
        plane[40:41, :] = jnp.where(part == 63, 0.0, pltpu.roll(plane[8:9, :], 127, 1))

    def ready(now, old, kept, other, turned_now, plane):
        own = plane[9:41, :] + plane[7:39, :] + turned_now - 4.0 * now
        rest = 2.0 * now - old + STEP_SQ * (other - (kept[0] + kept[1] + kept[2]))
        return own, rest

    def round0(k, adjoint):
        slot = lax.rem(k, 2)
        copies = halo0(slot)
        drop(dst, swap(pick(src, xp)) * wgt[...], cx)
        rims(xp)
        x = xp[8:40, :]
        m = [m0[l] for l in range(SLS)]
        x_own, x_rest = ready(x, xold[...], m, cx[...], pltpu.roll(x, 64, 1), xp)
        if adjoint:
            drop(src, swap(pick(dst, vp) * wgt[...]), cv)
            rims(vp)

            @pl.when(k == 2)
            def _():
                bulk(s_b, r_b, 3, 2).wait_recv()
                four = unpack(r_b, 0, 1)
                for n in range(4):
                    adj0[4 - n] = four[n * 32 : n * 32 + 32]
                adj0[0] = unpack2(r_b, 2)[0]

            n = STEPS - 2 - k
            v = vp[8:40, :]
            p = [p0[l] for l in range(SLS)]
            v_own, v_rest = ready(v, vold[...], p, cv[...] + adj0[n], pltpu.roll(v, 64, 1), vp)
        recv_all(copies)
        from_l, from_r = f_l[slot], f_r[slot]
        lap = x_own + jnp.where(low, from_l, pltpu.roll(from_r, 64, 1))
        force = mod0[...] * lap
        fresh = x_rest + STEP_SQ * force
        if adjoint:
            v_force = mod0[...] * (v_own + jnp.where(low, pltpu.roll(from_l, 64, 1), from_r))
            v_fresh = v_rest + STEP_SQ * v_force
            show(1 - slot, fresh, v_fresh)
        lap0[k] = lap
        xold[...] = x
        xp[8:40, :] = fresh
        if adjoint:
            for l in range(SLS):
                mem0[k, l] = m[l]
                m0[l] = RELAX[l] * m[l] + q0[l] * force
                p0[l] = RELAX[l] * p[l] + q0[l] * v_force
            vold[...] = v
            vp[8:40, :] = v_fresh
            vel0[n] = v_fresh
        sent_all(copies)

    def step0(k, carry):
        @pl.when(k == 3)
        def _():
            start_all(halo1)

        round0(k, True)
        return carry

    lax.fori_loop(0, STEPS - 1, step0, 0)

    def terms(vel, lap, mem, count):
        mu = zero
        q = [zero] * SLS
        for n in range(count):
            mu = mu + vel(n) * lap(n)
            for l in range(SLS):
                q[l] = q[l] + vel(n) * mem(n, l)
        return mu, q

    mu, _ = terms(lambda n: vel0[n], lambda n: lap0[n], lambda n, l: zero, STEPS - 1)
    q = [zero] * SLS
    for n in range(STEPS):
        for l in range(SLS):
            q[l] = q[l] + vel0[n] * (mem0[n, l] if n < STEPS - 1 else m0[l])
    turn = jnp.concatenate([mu] + q, axis=0).T
    s_o[pl.ds(0, parts, stride=8), :] = turn[0:64]
    s_o[pl.ds(1, parts, stride=8), :] = turn[64:128]
    spread(s_o, r_o, 2, 3, False)

    round0(STEPS - 1, False)

    turn = jnp.concatenate([xp[8:40, :], vel0[STEPS - 1] * lap0[STEPS - 1], zero, zero], axis=0).T
    s_e[pl.ds(0, parts, stride=8), :] = jnp.where(
        wide[0:64], turn[0:64], pltpu.roll(turn[64:128], 64, 1)
    )
    spread(s_e, r_e, 1, 4, False)

    recv_all(halo1)
    inner = lax.rem(lax.broadcasted_iota(jnp.int32, (EDGE, 128), 1), 32) < 16
    blank = jnp.zeros((128 - 2 * EDGE, 128), F32)

    def beside_planes(tiles):
        return jnp.concatenate([tiles[1], blank, tiles[0]], axis=0).T.reshape(4, 32, 128)

    for t in range(SENT // 4):
        four = slice(4 * t, 4 * t + 4)
        ext[1, four, core, :] = beside_planes([r_col[side, 1, t] for side in range(2)])
        ends = beside_planes(
            [jnp.where(inner, r_col[side, 2, t], r_col[side, 0, t]) for side in range(2)]
        )
        ext[1, four, 0:EDGE, :] = ends[:, 32 - EDGE :, :]
        ext[1, four, EDGE + 32 : 2 * EDGE + 32, :] = ends[:, 0:EDGE, :]
    sent_all(halo1)
    for c in range(2):
        for t in range(2):
            zp[c, t, 8:56, :] = ext[t, NOW + c]
            zp[c + 2, t, 8:56, :] = STEP_SQ * ext[t, ADJ + c]
            zold[c, t] = ext[t, PREV + c]
        vel1[STEPS, c] = STEP_SQ * ext[0, ADJ + c, core, :]

    rim = lax.broadcasted_iota(jnp.int32, (48, 128), 1)

    def around(f):
        main, side = zp[f, 0, 8:56, :], zp[f, 1, 8:56, :]
        lap = []
        ahead = [pltpu.roll(a, 127, 1) for a in (main, side)]
        behind = [pltpu.roll(a, 1, 1) for a in (main, side)]
        for t, centre in enumerate((main, side)):
            lap.append(
                zp[f, t, 9:57, :]
                + zp[f, t, 7:55, :]
                + jnp.where(rim == 127, ahead[1 - t], ahead[t])
                + jnp.where(rim == 0, behind[1 - t], behind[t])
                - 4.0 * centre
            )
        return (main, side), lap

    def round1(k, carry):
        n = STEPS - 2 - k
        source = ADJ + 2 * jnp.minimum(k + 1, STEPS - 1)
        for c in range(2):
            now, lap = around(c)
            lap1[k, c] = lap[0][8:40]
            for l in range(SLS):
                mem1[k, l, c] = ext[0, MEM + 2 * l + c, core, :]
            for t in range(2):
                kept = [ext[t, MEM + 2 * l + c] for l in range(SLS)]
                force = ext[t, MOD] * lap[t]
                accel = force - (kept[0] + kept[1] + kept[2])
                fresh = 2.0 * now[t] - zold[c, t] + STEP_SQ * accel
                for l in range(SLS):
                    ext[t, MEM + 2 * l + c] = RELAX[l] * kept[l] + ext[t, QW + l] * force
                zold[c, t] = now[t]
                zp[c, t, 8:56, :] = fresh
            now, lap = around(c + 2)
            for t in range(2):
                kept = [p1[l, c, t] for l in range(SLS)]
                force = ext[t, MOD] * lap[t]
                accel = force - (kept[0] + kept[1] + kept[2]) + ext[t, source + c]
                fresh = 2.0 * now[t] - zold[c + 2, t] + STEP_SQ * accel
                for l in range(SLS):
                    p1[l, c, t] = RELAX[l] * kept[l] + ext[t, QW + l] * force
                zold[c + 2, t] = now[t]
                zp[c + 2, t, 8:56, :] = fresh
                if t == 0:
                    vel1[n + 1, c] = fresh[8:40]
        return carry

    lax.fori_loop(0, STEPS, round1, 0)

    mu_sum, q_sum = zero, [zero] * SLS
    for c in range(2):
        o_u[c + 1] = zp[c, 0, 16:48, :]
        mu, q = terms(
            lambda n: vel1[n + 1, c], lambda n: lap1[n, c], lambda n, l: mem1[n, l, c], STEPS
        )
        mu_sum = mu_sum + mu
        q_sum = [a + b for a, b in zip(q_sum, q)]
    o_mu[...] = mu_sum
    for l in range(SLS):
        o_q[l] = q_sum[l]

    bulk(s_o, r_o, 2, 3).wait_recv()
    flip[pl.ds(0, parts, stride=2), :] = r_o[pl.ds(0, parts, stride=8), :]
    flip[pl.ds(1, parts, stride=2), :] = r_o[pl.ds(1, parts, stride=8), :]
    four = flip[...].T
    scale = 1.0 / (3.0 * STEPS)
    mu = o_mu[...] + four[0:32]
    for l in range(SLS):
        o_q[l] = (o_q[l] + four[32 + 32 * l : 64 + 32 * l]) * scale
    bulk(s_e, r_e, 1, 4).wait_recv()
    ends = r_e[pl.ds(0, parts, stride=8), :]
    flip[pl.ds(0, parts, stride=2), :] = ends
    flip[pl.ds(1, parts, stride=2), :] = pltpu.roll(ends, 64, 1)
    four = flip[...].T
    o_u[0] = four[0:32]
    o_mu[...] = (mu + four[32:64]) * scale

    bulk(s_1, r_1, 1, 0).wait_send()
    bulk(s_2, r_2, 5, 1).wait_send()
    bulk(s_b, r_b, 3, 2).wait_send()
    tables.wait_send()
    bulk(s_o, r_o, 2, 3).wait_send()
    bulk(s_e, r_e, 1, 4).wait_send()


def solution(mesh):
    groups, parts = mesh.shape["group"], mesh.shape["dom"]

    def shards(
        u_prev, u_now, memory, modulus, q_weight, adjoint_source, couple_src, couple_dst, couple_weight
    ):
        tables = [t.reshape(parts, -1).T for t in (couple_src, couple_dst, couple_weight)]
        plane = (32, 128)
        square = (128, 128)

        def vmem(*shape):
            return pltpu.VMEM(shape, F32)

        dma = pltpu.SemaphoreType.DMA
        return pl.pallas_call(
            functools.partial(kernel, groups, parts),
            out_shape=(vmem(*u_now.shape), vmem(*modulus.shape), vmem(*q_weight.shape)),
            in_specs=[pl.BlockSpec(memory_space=pltpu.HBM)] * 9,
            out_specs=[pl.BlockSpec(memory_space=pltpu.VMEM)] * 3,
            scratch_shapes=[
                vmem(5 + STEPS, *plane),
                pltpu.VMEM((2, parts), jnp.int32),
                pltpu.VMEM((2, parts), jnp.int32),
                vmem(2, parts),
                vmem(*square),
            ]
            + [vmem(parts * 8, 128)] * 6
            + [vmem(8, 128), vmem(parts // RUN, RUN * 8, 128)]
            + [vmem(parts * 8, 128)] * 5
            + [
                vmem(*square),
                vmem(*square),
                vmem(*square),
                vmem(*plane),
                vmem(SLS, *plane),
                vmem(STEPS - 1, *plane),
                vmem(48, 128),
                vmem(48, 128),
                vmem(*plane),
                vmem(*plane),
                vmem(SLS, *plane),
                vmem(SLS, *plane),
                vmem(*plane),
                vmem(*plane),
                vmem(STEPS, *plane),
                vmem(STEPS, *plane),
                vmem(STEPS, SLS, *plane),
                vmem(2, *plane),
                vmem(2, *plane),
                vmem(2, *plane),
                vmem(2, *plane),
                vmem(2, SENT + 2, 48, 128),
                vmem(4, 2, 64, 128),
                vmem(4, 2, 48, 128),
                vmem(SLS, 2, 2, 48, 128),
                vmem(STEPS, 2, *plane),
                vmem(STEPS + 1, 2, *plane),
                vmem(STEPS, SLS, 2, *plane),
                vmem(2, SENT // 4, EDGE, 128),
                vmem(2, 3, SENT // 4, EDGE, 128),
                dma((22,)),
                dma((5,)),
                dma((5,)),
                dma((2, 2)),
                dma((2, 2)),
                dma((6,)),
                dma((6,)),
                dma((2,)),
                dma((2,)),
                dma((RUN,)),
                dma((RUN,)),
            ],
            compiler_params=pltpu.CompilerParams(
                collective_id=0, has_side_effects=True, vmem_limit_bytes=60 * 1024 * 1024
            ),
        )(u_prev, u_now, memory, modulus, q_weight, adjoint_source, *tables)

    in_specs = (
        P(None, "dom", "group"),
        P(None, "dom", "group"),
        P(None, None, "dom", "group"),
        P("dom", "group"),
        P(None, "dom", "group"),
        P(None, None, "dom", "group"),
        P("group", "dom", None, None),
        P("group", "dom", None, None),
        P("group", "dom", None, None),
    )
    out_specs = (P(None, "dom", "group"), P("dom", "group"), P(None, "dom", "group"))
    return jax.shard_map(shards, mesh=mesh, in_specs=in_specs, out_specs=out_specs, check_vma=False)
```

```python
import functools

import jax
import jax.numpy as jnp
from jax import lax
from jax.experimental import pallas as pl
from jax.experimental.pallas import tpu as pltpu
from jax.sharding import PartitionSpec as P

MESH = pl.DeviceIdType.MESH
F32 = jnp.float32
SLS = 3
STEPS = 8
RELAX = (0.6, 0.85, 0.97)
STEP_SQ = 0.25
RUN = 4
HALF = 8
EDGE = 8
SENT = 28
NOW, PREV, MEM, MOD, QW, ADJ = 0, 2, 4, 10, 11, 14


def snake(g, d):
    row, col = lax.div(d, RUN), lax.rem(d, RUN)
    flip = lax.rem(row + (g < HALF).astype(jnp.int32), 2) == 1
    return row * RUN + jnp.where(flip, RUN - 1 - col, col)


def kernel(
    groups,
    parts,
    up_h,
    un_h,
    mem_h,
    mod_h,
    q_h,
    adj_h,
    src_h,
    dst_h,
    wgt_h,
    o_u,
    o_mu,
    o_q,
    i0,
    isrc,
    idst,
    iwgt,
    flip,
    s_1,
    r_1,
    s_2,
    r_2,
    s_b,
    r_b,
    s_q,
    r_q,
    s_t,
    r_t,
    flat,
    s_o,
    r_o,
    s_e,
    r_e,
    src,
    dst,
    wgt,
    mod0,
    q0,
    adj0,
    xp,
    vp,
    xold,
    vold,
    m0,
    p0,
    cx,
    cv,
    fx,
    fv,
    lap0,
    vel0,
    mem0,
    s_l,
    s_r,
    f_l,
    f_r,
    ext,
    zp,
    zold,
    p1,
    lap1,
    vel1,
    mem1,
    s_col,
    r_col,
    in_sem,
    bulk_send,
    bulk_recv,
    side_send,
    side_recv,
    col_send,
    col_recv,
    row_send,
    row_recv,
    tab_send,
    tab_recv,
):
    g, d = lax.axis_index("group"), lax.axis_index("dom")
    last = parts - 1
    turned = lax.rem(g, 2) == 1

    def turn_pos(n):
        return jnp.where(turned, last - n, n)

    place = snake(g, d)
    pos = turn_pos(place)
    has_lo, has_hi = g > 0, g < groups - 1
    at_top, at_end = d > 0, d < last
    first, final = pos == 0, pos == last
    at_left = jnp.logical_or(jnp.logical_not(first), has_lo)
    at_right = jnp.logical_or(jnp.logical_not(final), has_hi)
    prev = snake(g, jnp.maximum(place - 1, 0))
    after = snake(g, jnp.minimum(place + 1, last))
    lo_g, hi_g = jnp.maximum(g - 1, 0), jnp.minimum(g + 1, groups - 1)
    left = (
        jnp.where(first, lo_g, g),
        jnp.where(first, snake(lo_g, place), jnp.where(turned, after, prev)),
    )
    right = (
        jnp.where(final, hi_g, g),
        jnp.where(final, snake(hi_g, place), jnp.where(turned, prev, after)),
    )
    over_lo = jnp.logical_and(first, g == HALF)
    over_hi = jnp.logical_and(jnp.logical_and(final, has_hi), g == HALF - 1)

    def far(t):
        half = lax.div(t + 1, 2)
        step = jnp.where(lax.rem(t, 2) == 1, half, -half)
        return lax.rem(d + parts // 2 + step, parts)

    barrier = pltpu.get_barrier_semaphore()

    def hello(group, part):
        pl.semaphore_signal(barrier, inc=1, device_id=(group, part), device_id_type=MESH)

    def greet(t, carry):
        hello(g, far(t))
        return carry

    beside = []
    for away, group_there in ((-1, has_lo), (1, has_hi)):
        for step, part_there in ((-1, at_top), (0, True), (1, at_end)):
            there = group_there if part_there is True else jnp.logical_and(group_there, part_there)
            beside.append((away, step, there))
    guests = last + over_lo.astype(jnp.int32) + over_hi.astype(jnp.int32)
    for away, step, there in beside:
        pl.when(there)(functools.partial(hello, g + away, d + step))
        guests = guests + there.astype(jnp.int32)
    pl.when(over_lo)(functools.partial(hello, *left))
    pl.when(over_hi)(functools.partial(hello, *right))
    lax.fori_loop(0, last, greet, 0)

    core = pl.ds(EDGE, 32)
    pairs = [
        (un_h.at[0], i0.at[0]),
        (adj_h.at[:, 0], i0.at[pl.ds(5, STEPS)]),
        (src_h, isrc),
        (dst_h, idst),
        (wgt_h, iwgt),
        (up_h.at[0], i0.at[1]),
        (mem_h.at[:, 0], i0.at[pl.ds(2, SLS)]),
        (mod_h, ext.at[0, MOD, core]),
        (q_h, ext.at[0, pl.ds(QW, SLS), core]),
        (un_h.at[pl.ds(1, 2)], ext.at[0, pl.ds(NOW, 2), core]),
        (up_h.at[pl.ds(1, 2)], ext.at[0, pl.ds(PREV, 2), core]),
    ]
    for l in range(SLS):
        pairs.append((mem_h.at[l, pl.ds(1, 2)], ext.at[0, pl.ds(MEM + 2 * l, 2), core]))
    for n in range(STEPS):
        spot = ADJ + 2 * (STEPS - 1 - n)
        pairs.append((adj_h.at[n, pl.ds(1, 2)], ext.at[0, pl.ds(spot, 2), core]))
    loads = []
    for at, (source, target) in enumerate(pairs):
        loads.append(pltpu.make_async_copy(source, target, in_sem.at[at]))
        loads[-1].start()

    def clear(ref, *at):
        def run():
            ref[at] = jnp.zeros_like(ref[at])

        return run

    no = jnp.logical_not
    pl.when(no(at_left))(clear(f_l, slice(None)))
    pl.when(no(at_right))(clear(f_r, slice(None)))
    pl.when(no(at_top))(clear(ext, 0, slice(0, SENT), slice(0, EDGE)))
    pl.when(no(at_end))(clear(ext, 0, slice(0, SENT), slice(EDGE + 32, 2 * EDGE + 32)))
    for away, step, there in beside:
        pl.when(no(there))(clear(r_col, (away + 1) // 2, step + 1))
    zp[...] = jnp.zeros_like(zp)
    zold[...] = jnp.zeros_like(zold)
    p1[...] = jnp.zeros_like(p1)

    lane = lax.broadcasted_iota(jnp.int32, (32, 128), 1)
    low = lane < 64
    edge = lax.broadcasted_iota(jnp.int32, (128, 128), 1)
    wide = edge < 64
    zero = jnp.zeros((32, 128), F32)

    for load in loads:
        load.wait()

    def pack4(planes, target, row):
        flip[...] = jnp.concatenate(planes, axis=0).T
        target[pl.ds(row, parts, stride=8), :] = flip[pl.ds(0, parts, stride=2), :]
        target[pl.ds(row + 1, parts, stride=8), :] = flip[pl.ds(1, parts, stride=2), :]

    def pack2(planes, target, row):
        flip[...] = jnp.concatenate(planes + [zero, zero], axis=0).T
        target[pl.ds(row, parts, stride=8), :] = jnp.where(
            wide[0:64],
            flip[pl.ds(0, parts, stride=2), :],
            pltpu.roll(flip[pl.ds(1, parts, stride=2), :], 64, 1),
        )

    adj = 5
    pack2([i0[0], i0[adj + 7]], s_1, 0)
    for t, table in enumerate((isrc, idst, iwgt)):
        row = jnp.concatenate([table[0:1, :].astype(F32), table[1:2, :].astype(F32)], axis=1)
        s_t[t : t + 1, :] = row
    pack4([i0[1], i0[2], i0[3], i0[4]], s_2, 0)
    pack2([ext[0, MOD, core], i0[adj + 6]], s_2, 2)
    pack4([ext[0, QW, core], ext[0, QW + 1, core], ext[0, QW + 2, core], i0[adj + 5]], s_q, 0)
    pack4([i0[adj + 4], i0[adj + 3], i0[adj + 2], i0[adj + 1]], s_b, 0)
    pack2([i0[adj], zero], s_b, 2)

    for t in range(SENT // 4):
        tile = ext[0, 4 * t : 4 * t + 4, core, :].reshape(128, 128).T
        s_col[0, t] = tile[0:EDGE]
        s_col[1, t] = tile[128 - EDGE :]

    pl.semaphore_wait(barrier, guests)

    def spread(source, target, rows, which, by_pos):
        def send(t, carry):
            peer = far(t)
            take = turn_pos(snake(g, peer)) if by_pos else peer
            land = d if by_pos else pos
            pltpu.make_async_remote_copy(
                src_ref=source.at[pl.ds(pl.multiple_of(take * 8, 8), rows), :],
                dst_ref=target.at[pl.ds(pl.multiple_of(land * 8, 8), rows), :],
                send_sem=bulk_send.at[which],
                recv_sem=bulk_recv.at[which],
                device_id=(g, peer),
                device_id_type=MESH,
            ).start()
            return carry

        lax.fori_loop(0, last, send, 0)
        mine = pl.ds(pl.multiple_of((pos if by_pos else d) * 8, 8), 8)
        here = pl.ds(pl.multiple_of((d if by_pos else pos) * 8, 8), 8)
        target[here, :] = source[mine, :]

    def bulk(source, target, rows, which):
        return pltpu.make_async_remote_copy(
            src_ref=source.at[pl.ds(0, last * rows), :],
            dst_ref=target.at[pl.ds(0, last * rows), :],
            send_sem=bulk_send.at[which],
            recv_sem=bulk_recv.at[which],
            device_id=(g, lax.rem(d + 1, parts)),
            device_id_type=MESH,
        )

    def start_all(copies):
        for cond, copy, _ in copies:
            pl.when(cond)(copy.start)

    def recv_all(copies):
        for _, copy, cond in copies:
            pl.when(cond)(copy.wait_recv)

    def sent_all(copies):
        for cond, copy, _ in copies:
            pl.when(cond)(copy.wait_send)

    halo1 = []
    for at, (away, step, there) in enumerate(beside):
        side, back = (away + 1) // 2, len(beside) - 1 - at
        halo1.append(
            (
                there,
                pltpu.make_async_remote_copy(
                    src_ref=s_col.at[side],
                    dst_ref=r_col.at[1 - side, 1 - step],
                    send_sem=col_send.at[at],
                    recv_sem=col_recv.at[back],
                    device_id=(g + away, d + step),
                    device_id_type=MESH,
                ),
                beside[back][2],
            )
        )
    planes = pl.ds(0, SENT)
    for at, (step, there, source, target, other) in enumerate(
        ((-1, at_top, EDGE, EDGE + 32, at_end), (1, at_end, 32, 0, at_top))
    ):
        halo1.append(
            (
                there,
                pltpu.make_async_remote_copy(
                    src_ref=ext.at[0, planes, pl.ds(source, EDGE)],
                    dst_ref=ext.at[0, planes, pl.ds(target, EDGE)],
                    send_sem=row_send.at[at],
                    recv_sem=row_recv.at[at],
                    device_id=(g, d + step),
                    device_id_type=MESH,
                ),
                other,
            )
        )

    lines, depth = parts // RUN, 3
    line, spot = lax.div(d, RUN), lax.rem(d, RUN)
    slab = pl.ds(pl.multiple_of(spot * 8, 8), depth)

    def along(t, carry):
        half = lax.div(t + 1, 2)
        step = jnp.where(lax.rem(t, 2) == 1, half, -half)
        peer = lax.rem(line + lines // 2 + step, lines)
        pltpu.make_async_remote_copy(
            src_ref=s_t.at[pl.ds(0, depth)],
            dst_ref=r_t.at[line, slab],
            send_sem=tab_send.at[0],
            recv_sem=tab_recv.at[0],
            device_id=(g, peer * RUN + spot),
            device_id_type=MESH,
        ).start()
        return carry

    across = [
        pltpu.make_async_remote_copy(
            src_ref=r_t.at[:, slab],
            dst_ref=r_t.at[:, slab],
            send_sem=tab_send.at[step],
            recv_sem=tab_recv.at[step],
            device_id=(g, line * RUN + lax.rem(spot + step, RUN)),
            device_id_type=MESH,
        )
        for step in range(1, RUN)
    ]
    tables = pltpu.make_async_remote_copy(
        src_ref=r_t.at[pl.ds(0, lines - 1), pl.ds(0, depth)],
        dst_ref=r_t.at[pl.ds(0, lines - 1), pl.ds(0, depth)],
        send_sem=tab_send.at[0],
        recv_sem=tab_recv.at[0],
        device_id=(g, lax.rem(d + 1, parts)),
        device_id_type=MESH,
    )

    lax.fori_loop(0, lines - 1, along, 0)
    r_t[line, slab, :] = s_t[0:depth, :]
    spread(s_1, r_1, 1, 0, True)
    spread(s_2, r_2, 3, 1, True)
    spread(s_q, r_q, 2, 5, True)
    spread(s_b, r_b, 3, 2, True)

    def unpack(source, first, second):
        return jnp.concatenate(
            [
                source[pl.ds(first, parts, stride=8), :],
                source[pl.ds(second, parts, stride=8), :],
            ],
            axis=0,
        ).T

    def halo0(slot):
        return (
            (
                at_left,
                pltpu.make_async_remote_copy(
                    src_ref=s_l.at[slot],
                    dst_ref=f_r.at[slot],
                    send_sem=side_send.at[slot, 0],
                    recv_sem=side_recv.at[slot, 1],
                    device_id=left,
                    device_id_type=MESH,
                ),
                at_right,
            ),
            (
                at_right,
                pltpu.make_async_remote_copy(
                    src_ref=s_r.at[slot],
                    dst_ref=f_l.at[slot],
                    send_sem=side_send.at[slot, 1],
                    recv_sem=side_recv.at[slot, 0],
                    device_id=right,
                    device_id_type=MESH,
                ),
                at_left,
            ),
        )

    def show(slot, x, v):
        s_l[slot] = jnp.where(low, x, pltpu.roll(v, 64, 1))
        s_r[slot] = jnp.where(low, pltpu.roll(x, 64, 1), v)
        start_all(halo0(slot))

    def unpack2(source, row):
        both = unpack(source, row, row)
        return [jnp.where(low, both[at : at + 32], both[at + 64 : at + 96]) for at in (0, 32)]

    tables.wait_recv()
    for copy in across:
        copy.start()
    bulk(s_1, r_1, 1, 0).wait_recv()
    x, v = unpack2(r_1, 0)
    v = STEP_SQ * v
    show(0, x, v)
    xp[8:40, :] = x
    vp[8:40, :] = v
    vel0[STEPS - 1] = v
    vold[...] = zero
    for l in range(SLS):
        p0[l] = zero

    for copy in across:
        copy.wait()
    flat[...] = r_t[...].reshape(parts * 8, 128)
    src[...] = unpack(flat, 0, 0)
    dst[...] = unpack(flat, 1, 1)
    wgt[...] = unpack(flat, 2, 2)
    bulk(s_2, r_2, 3, 1).wait_recv()
    four = unpack(r_2, 0, 1)
    xold[...] = four[0:32]
    for l in range(SLS):
        m0[l] = four[32 + 32 * l : 64 + 32 * l]
    mod0[...], adj0[6] = unpack2(r_2, 2)

    def swap(a):
        t = a.T
        top, bottom = t[0:64], t[64:128]
        half = wide[0:64]
        return jnp.concatenate(
            [
                jnp.where(half, top, pltpu.roll(bottom, 64, 1)),
                jnp.where(half, pltpu.roll(top, 64, 1), bottom),
            ],
            axis=0,
        )

    def pick(table, plane):
        rows = table[...]
        out = jnp.zeros((128, 128), F32)
        for r in range(32):
            out = jnp.where(rows == float(r), plane[8 + r : 9 + r, :], out)
        return out

    def drop(table, values, out):
        rows = table[...]
        for r in range(32):
            out[r : r + 1, :] = jnp.sum(
                jnp.where(rows == float(r), values, 0.0), axis=0, keepdims=True
            )

    part = lax.rem(lax.broadcasted_iota(jnp.int32, (1, 128), 1), 64)

    def rims(plane):
        plane[7:8, :] = jnp.where(part == 0, 0.0, pltpu.roll(plane[39:40, :], 1, 1))
        plane[40:41, :] = jnp.where(part == 63, 0.0, pltpu.roll(plane[8:9, :], 127, 1))

    def ready(now, old, kept, other, turned_now, plane):
        own = plane[9:41, :] + plane[7:39, :] + turned_now - 4.0 * now
        rest = 2.0 * now - old + STEP_SQ * (other - (kept[0] + kept[1] + kept[2]))
        return own, rest

    def absorb(k, adjoint):
        for l in range(SLS):
            mem0[k - 1, l] = m0[l]
            m0[l] = RELAX[l] * m0[l] + q0[l] * fx[...]
            if adjoint:
                p0[l] = RELAX[l] * p0[l] + q0[l] * fv[...]

    def round0(k, adjoint):
        slot = lax.rem(k, 2)
        copies = halo0(slot)
        drop(dst, swap(pick(src, xp)) * wgt[...], cx)
        rims(xp)
        if adjoint:
            drop(src, swap(pick(dst, vp) * wgt[...]), cv)
            rims(vp)
        if adjoint:

            @pl.when(k == 1)
            def _():
                bulk(s_q, r_q, 2, 5).wait_recv()
                four = unpack(r_q, 0, 1)
                for l in range(SLS):
                    q0[l] = four[32 * l : 32 * l + 32]
                adj0[5] = four[96:128]

            @pl.when(k > 0)
            def _():
                absorb(k, True)

        x = xp[8:40, :]
        m = [m0[l] for l in range(SLS)]
        x_own, x_rest = ready(x, xold[...], m, cx[...], pltpu.roll(x, 64, 1), xp)
        if adjoint:

            @pl.when(k == 2)
            def _():
                bulk(s_b, r_b, 3, 2).wait_recv()
                four = unpack(r_b, 0, 1)
                for n in range(4):
                    adj0[4 - n] = four[n * 32 : n * 32 + 32]
                adj0[0] = unpack2(r_b, 2)[0]

            n = STEPS - 2 - k
            v = vp[8:40, :]
            p = [p0[l] for l in range(SLS)]
            v_own, v_rest = ready(v, vold[...], p, cv[...] + adj0[n], pltpu.roll(v, 64, 1), vp)
        recv_all(copies)
        from_l, from_r = f_l[slot], f_r[slot]
        lap = x_own + jnp.where(low, from_l, pltpu.roll(from_r, 64, 1))
        force = mod0[...] * lap
        fresh = x_rest + STEP_SQ * force
        if adjoint:
            v_force = mod0[...] * (v_own + jnp.where(low, pltpu.roll(from_l, 64, 1), from_r))
            v_fresh = v_rest + STEP_SQ * v_force
            show(1 - slot, fresh, v_fresh)
        lap0[k] = lap
        xold[...] = x
        xp[8:40, :] = fresh
        if adjoint:
            fx[...] = force
            fv[...] = v_force
            vold[...] = v
            vp[8:40, :] = v_fresh
            vel0[n] = v_fresh
        sent_all(copies)

    def step0(k, carry):
        @pl.when(k == 4)
        def _():
            start_all(halo1)

        round0(k, True)
        return carry

    lax.fori_loop(0, STEPS - 1, step0, 0)
    absorb(STEPS - 1, False)

    def terms(vel, lap, mem, count):
        mu = zero
        q = [zero] * SLS
        for n in range(count):
            mu = mu + vel(n) * lap(n)
            for l in range(SLS):
                q[l] = q[l] + vel(n) * mem(n, l)
        return mu, q

    mu, _ = terms(lambda n: vel0[n], lambda n: lap0[n], lambda n, l: zero, STEPS - 1)
    q = [zero] * SLS
    for n in range(STEPS):
        for l in range(SLS):
            q[l] = q[l] + vel0[n] * (mem0[n, l] if n < STEPS - 1 else m0[l])
    turn = jnp.concatenate([mu] + q, axis=0).T
    s_o[pl.ds(0, parts, stride=8), :] = turn[0:64]
    s_o[pl.ds(1, parts, stride=8), :] = turn[64:128]
    spread(s_o, r_o, 2, 3, False)

    round0(STEPS - 1, False)

    turn = jnp.concatenate([xp[8:40, :], vel0[STEPS - 1] * lap0[STEPS - 1], zero, zero], axis=0).T
    s_e[pl.ds(0, parts, stride=8), :] = jnp.where(
        wide[0:64], turn[0:64], pltpu.roll(turn[64:128], 64, 1)
    )
    spread(s_e, r_e, 1, 4, False)

    recv_all(halo1)
    inner = lax.rem(lax.broadcasted_iota(jnp.int32, (EDGE, 128), 1), 32) < 16
    blank = jnp.zeros((128 - 2 * EDGE, 128), F32)

    def beside_planes(tiles):
        return jnp.concatenate([tiles[1], blank, tiles[0]], axis=0).T.reshape(4, 32, 128)

    for t in range(SENT // 4):
        four = slice(4 * t, 4 * t + 4)
        ext[1, four, core, :] = beside_planes([r_col[side, 1, t] for side in range(2)])
        ends = beside_planes(
            [jnp.where(inner, r_col[side, 2, t], r_col[side, 0, t]) for side in range(2)]
        )
        ext[1, four, 0:EDGE, :] = ends[:, 32 - EDGE :, :]
        ext[1, four, EDGE + 32 : 2 * EDGE + 32, :] = ends[:, 0:EDGE, :]
    sent_all(halo1)
    for c in range(2):
        for t in range(2):
            zp[c, t, 8:56, :] = ext[t, NOW + c]
            zp[c + 2, t, 8:56, :] = STEP_SQ * ext[t, ADJ + c]
            zold[c, t] = ext[t, PREV + c]
        vel1[STEPS, c] = STEP_SQ * ext[0, ADJ + c, core, :]

    rim = lax.broadcasted_iota(jnp.int32, (48, 128), 1)

    def around(f):
        main, side = zp[f, 0, 8:56, :], zp[f, 1, 8:56, :]
        lap = []
        ahead = [pltpu.roll(a, 127, 1) for a in (main, side)]
        behind = [pltpu.roll(a, 1, 1) for a in (main, side)]
        for t, centre in enumerate((main, side)):
            lap.append(
                zp[f, t, 9:57, :]
                + zp[f, t, 7:55, :]
                + jnp.where(rim == 127, ahead[1 - t], ahead[t])
                + jnp.where(rim == 0, behind[1 - t], behind[t])
                - 4.0 * centre
            )
        return (main, side), lap

    def round1(k, carry):
        n = STEPS - 2 - k
        source = ADJ + 2 * jnp.minimum(k + 1, STEPS - 1)
        for c in range(2):
            now, lap = around(c)
            lap1[k, c] = lap[0][8:40]
            for l in range(SLS):
                mem1[k, l, c] = ext[0, MEM + 2 * l + c, core, :]
            for t in range(2):
                kept = [ext[t, MEM + 2 * l + c] for l in range(SLS)]
                force = ext[t, MOD] * lap[t]
                accel = force - (kept[0] + kept[1] + kept[2])
                fresh = 2.0 * now[t] - zold[c, t] + STEP_SQ * accel
                for l in range(SLS):
                    ext[t, MEM + 2 * l + c] = RELAX[l] * kept[l] + ext[t, QW + l] * force
                zold[c, t] = now[t]
                zp[c, t, 8:56, :] = fresh
            now, lap = around(c + 2)
            for t in range(2):
                kept = [p1[l, c, t] for l in range(SLS)]
                force = ext[t, MOD] * lap[t]
                accel = force - (kept[0] + kept[1] + kept[2]) + ext[t, source + c]
                fresh = 2.0 * now[t] - zold[c + 2, t] + STEP_SQ * accel
                for l in range(SLS):
                    p1[l, c, t] = RELAX[l] * kept[l] + ext[t, QW + l] * force
                zold[c + 2, t] = now[t]
                zp[c + 2, t, 8:56, :] = fresh
                if t == 0:
                    vel1[n + 1, c] = fresh[8:40]
        return carry

    lax.fori_loop(0, STEPS, round1, 0)

    mu_sum, q_sum = zero, [zero] * SLS
    for c in range(2):
        o_u[c + 1] = zp[c, 0, 16:48, :]
        mu, q = terms(
            lambda n: vel1[n + 1, c], lambda n: lap1[n, c], lambda n, l: mem1[n, l, c], STEPS
        )
        mu_sum = mu_sum + mu
        q_sum = [a + b for a, b in zip(q_sum, q)]
    o_mu[...] = mu_sum
    for l in range(SLS):
        o_q[l] = q_sum[l]

    bulk(s_o, r_o, 2, 3).wait_recv()
    flip[pl.ds(0, parts, stride=2), :] = r_o[pl.ds(0, parts, stride=8), :]
    flip[pl.ds(1, parts, stride=2), :] = r_o[pl.ds(1, parts, stride=8), :]
    four = flip[...].T
    scale = 1.0 / (3.0 * STEPS)
    mu = o_mu[...] + four[0:32]
    for l in range(SLS):
        o_q[l] = (o_q[l] + four[32 + 32 * l : 64 + 32 * l]) * scale
    bulk(s_e, r_e, 1, 4).wait_recv()
    ends = r_e[pl.ds(0, parts, stride=8), :]
    flip[pl.ds(0, parts, stride=2), :] = ends
    flip[pl.ds(1, parts, stride=2), :] = pltpu.roll(ends, 64, 1)
    four = flip[...].T
    o_u[0] = four[0:32]
    o_mu[...] = (mu + four[32:64]) * scale

    bulk(s_1, r_1, 1, 0).wait_send()
    bulk(s_2, r_2, 3, 1).wait_send()
    bulk(s_q, r_q, 2, 5).wait_send()
    bulk(s_b, r_b, 3, 2).wait_send()
    tables.wait_send()
    bulk(s_o, r_o, 2, 3).wait_send()
    bulk(s_e, r_e, 1, 4).wait_send()


def solution(mesh):
    groups, parts = mesh.shape["group"], mesh.shape["dom"]

    def shards(
        u_prev, u_now, memory, modulus, q_weight, adjoint_source, couple_src, couple_dst, couple_weight
    ):
        tables = [t.reshape(parts, -1).T for t in (couple_src, couple_dst, couple_weight)]
        plane = (32, 128)
        square = (128, 128)

        def vmem(*shape):
            return pltpu.VMEM(shape, F32)

        dma = pltpu.SemaphoreType.DMA
        return pl.pallas_call(
            functools.partial(kernel, groups, parts),
            out_shape=(vmem(*u_now.shape), vmem(*modulus.shape), vmem(*q_weight.shape)),
            in_specs=[pl.BlockSpec(memory_space=pltpu.HBM)] * 9,
            out_specs=[pl.BlockSpec(memory_space=pltpu.VMEM)] * 3,
            scratch_shapes=[
                vmem(5 + STEPS, *plane),
                pltpu.VMEM((2, parts), jnp.int32),
                pltpu.VMEM((2, parts), jnp.int32),
                vmem(2, parts),
                vmem(*square),
            ]
            + [vmem(parts * 8, 128)] * 8
            + [vmem(8, 128), vmem(parts // RUN, RUN * 8, 128)]
            + [vmem(parts * 8, 128)] * 5
            + [
                vmem(*square),
                vmem(*square),
                vmem(*square),
                vmem(*plane),
                vmem(SLS, *plane),
                vmem(STEPS - 1, *plane),
                vmem(48, 128),
                vmem(48, 128),
                vmem(*plane),
                vmem(*plane),
                vmem(SLS, *plane),
                vmem(SLS, *plane),
                vmem(*plane),
                vmem(*plane),
                vmem(*plane),
                vmem(*plane),
                vmem(STEPS, *plane),
                vmem(STEPS, *plane),
                vmem(STEPS, SLS, *plane),
                vmem(2, *plane),
                vmem(2, *plane),
                vmem(2, *plane),
                vmem(2, *plane),
                vmem(2, SENT + 2, 48, 128),
                vmem(4, 2, 64, 128),
                vmem(4, 2, 48, 128),
                vmem(SLS, 2, 2, 48, 128),
                vmem(STEPS, 2, *plane),
                vmem(STEPS + 1, 2, *plane),
                vmem(STEPS, SLS, 2, *plane),
                vmem(2, SENT // 4, EDGE, 128),
                vmem(2, 3, SENT // 4, EDGE, 128),
                dma((22,)),
                dma((6,)),
                dma((6,)),
                dma((2, 2)),
                dma((2, 2)),
                dma((6,)),
                dma((6,)),
                dma((2,)),
                dma((2,)),
                dma((RUN,)),
                dma((RUN,)),
            ],
            compiler_params=pltpu.CompilerParams(
                collective_id=0, has_side_effects=True, vmem_limit_bytes=60 * 1024 * 1024
            ),
        )(u_prev, u_now, memory, modulus, q_weight, adjoint_source, *tables)

    in_specs = (
        P(None, "dom", "group"),
        P(None, "dom", "group"),
        P(None, None, "dom", "group"),
        P("dom", "group"),
        P(None, "dom", "group"),
        P(None, None, "dom", "group"),
        P("group", "dom", None, None),
        P("group", "dom", None, None),
        P("group", "dom", None, None),
    )
    out_specs = (P(None, "dom", "group"), P("dom", "group"), P(None, "dom", "group"))
    return jax.shard_map(shards, mesh=mesh, in_specs=in_specs, out_specs=out_specs, check_vma=False)
```

```python
import functools

import jax
import jax.numpy as jnp
from jax import lax
from jax.experimental import pallas as pl
from jax.experimental.pallas import tpu as pltpu
from jax.sharding import PartitionSpec as P

MESH = pl.DeviceIdType.MESH
F32 = jnp.float32
SLS = 3
STEPS = 8
RELAX = (0.6, 0.85, 0.97)
STEP_SQ = 0.25
RUN = 4
HALF = 8
EDGE = 8
SENT = 28
NOW, PREV, MEM, MOD, QW, ADJ = 0, 2, 4, 10, 11, 14


def snake(g, d):
    row, col = lax.div(d, RUN), lax.rem(d, RUN)
    flip = lax.rem(row + (g < HALF).astype(jnp.int32), 2) == 1
    return row * RUN + jnp.where(flip, RUN - 1 - col, col)


def kernel(
    groups,
    parts,
    up_h,
    un_h,
    mem_h,
    mod_h,
    q_h,
    adj_h,
    src_h,
    dst_h,
    wgt_h,
    o_u,
    o_mu,
    o_q,
    i0,
    isrc,
    idst,
    iwgt,
    flip,
    s_1,
    r_1,
    s_2,
    r_2,
    s_b,
    r_b,
    s_q,
    r_q,
    s_c,
    r_c,
    s_t,
    r_t,
    flat,
    s_o,
    r_o,
    s_e,
    r_e,
    src,
    dst,
    wgt,
    mod0,
    q0,
    adj0,
    xp,
    vp,
    xold,
    vold,
    m0,
    p0,
    cx,
    cv,
    fx,
    fv,
    lap0,
    vel0,
    mem0,
    s_l,
    s_r,
    f_l,
    f_r,
    ext,
    zp,
    zold,
    p1,
    lap1,
    vel1,
    mem1,
    s_col,
    r_col,
    in_sem,
    bulk_send,
    bulk_recv,
    side_send,
    side_recv,
    col_send,
    col_recv,
    row_send,
    row_recv,
    tab_send,
    tab_recv,
):
    g, d = lax.axis_index("group"), lax.axis_index("dom")
    last = parts - 1
    turned = lax.rem(g, 2) == 1

    def turn_pos(n):
        return jnp.where(turned, last - n, n)

    place = snake(g, d)
    pos = turn_pos(place)
    has_lo, has_hi = g > 0, g < groups - 1
    at_top, at_end = d > 0, d < last
    first, final = pos == 0, pos == last
    at_left = jnp.logical_or(jnp.logical_not(first), has_lo)
    at_right = jnp.logical_or(jnp.logical_not(final), has_hi)
    prev = snake(g, jnp.maximum(place - 1, 0))
    after = snake(g, jnp.minimum(place + 1, last))
    lo_g, hi_g = jnp.maximum(g - 1, 0), jnp.minimum(g + 1, groups - 1)
    left = (
        jnp.where(first, lo_g, g),
        jnp.where(first, snake(lo_g, place), jnp.where(turned, after, prev)),
    )
    right = (
        jnp.where(final, hi_g, g),
        jnp.where(final, snake(hi_g, place), jnp.where(turned, prev, after)),
    )
    over_lo = jnp.logical_and(first, g == HALF)
    over_hi = jnp.logical_and(jnp.logical_and(final, has_hi), g == HALF - 1)

    def far(t):
        half = lax.div(t + 1, 2)
        step = jnp.where(lax.rem(t, 2) == 1, half, -half)
        return lax.rem(d + parts // 2 + step, parts)

    barrier = pltpu.get_barrier_semaphore()

    def hello(group, part):
        pl.semaphore_signal(barrier, inc=1, device_id=(group, part), device_id_type=MESH)

    def greet(t, carry):
        hello(g, far(t))
        return carry

    beside = []
    for away, group_there in ((-1, has_lo), (1, has_hi)):
        for step, part_there in ((-1, at_top), (0, True), (1, at_end)):
            there = group_there if part_there is True else jnp.logical_and(group_there, part_there)
            beside.append((away, step, there))
    guests = last + over_lo.astype(jnp.int32) + over_hi.astype(jnp.int32)
    for away, step, there in beside:
        pl.when(there)(functools.partial(hello, g + away, d + step))
        guests = guests + there.astype(jnp.int32)
    pl.when(over_lo)(functools.partial(hello, *left))
    pl.when(over_hi)(functools.partial(hello, *right))
    lax.fori_loop(0, last, greet, 0)

    core = pl.ds(EDGE, 32)
    pairs = [
        (un_h.at[0], i0.at[0]),
        (adj_h.at[:, 0], i0.at[pl.ds(5, STEPS)]),
        (src_h, isrc),
        (dst_h, idst),
        (wgt_h, iwgt),
        (up_h.at[0], i0.at[1]),
        (mem_h.at[:, 0], i0.at[pl.ds(2, SLS)]),
        (mod_h, ext.at[0, MOD, core]),
        (q_h, ext.at[0, pl.ds(QW, SLS), core]),
        (un_h.at[pl.ds(1, 2)], ext.at[0, pl.ds(NOW, 2), core]),
        (up_h.at[pl.ds(1, 2)], ext.at[0, pl.ds(PREV, 2), core]),
    ]
    for l in range(SLS):
        pairs.append((mem_h.at[l, pl.ds(1, 2)], ext.at[0, pl.ds(MEM + 2 * l, 2), core]))
    for n in range(STEPS):
        spot = ADJ + 2 * (STEPS - 1 - n)
        pairs.append((adj_h.at[n, pl.ds(1, 2)], ext.at[0, pl.ds(spot, 2), core]))
    loads = []
    for at, (source, target) in enumerate(pairs):
        loads.append(pltpu.make_async_copy(source, target, in_sem.at[at]))
        loads[-1].start()

    def clear(ref, *at):
        def run():
            ref[at] = jnp.zeros_like(ref[at])

        return run

    no = jnp.logical_not
    pl.when(no(at_left))(clear(f_l, slice(None)))
    pl.when(no(at_right))(clear(f_r, slice(None)))
    pl.when(no(at_top))(clear(ext, 0, slice(0, SENT), slice(0, EDGE)))
    pl.when(no(at_end))(clear(ext, 0, slice(0, SENT), slice(EDGE + 32, 2 * EDGE + 32)))
    for away, step, there in beside:
        pl.when(no(there))(clear(r_col, (away + 1) // 2, step + 1))
    zp[...] = jnp.zeros_like(zp)
    zold[...] = jnp.zeros_like(zold)
    p1[...] = jnp.zeros_like(p1)

    lane = lax.broadcasted_iota(jnp.int32, (32, 128), 1)
    low = lane < 64
    edge = lax.broadcasted_iota(jnp.int32, (128, 128), 1)
    wide = edge < 64
    zero = jnp.zeros((32, 128), F32)

    for load in loads:
        load.wait()

    def pack4(planes, target, row):
        flip[...] = jnp.concatenate(planes, axis=0).T
        target[pl.ds(row, parts, stride=8), :] = flip[pl.ds(0, parts, stride=2), :]
        target[pl.ds(row + 1, parts, stride=8), :] = flip[pl.ds(1, parts, stride=2), :]

    def pack2(planes, target, row):
        flip[...] = jnp.concatenate(planes + [zero, zero], axis=0).T
        target[pl.ds(row, parts, stride=8), :] = jnp.where(
            wide[0:64],
            flip[pl.ds(0, parts, stride=2), :],
            pltpu.roll(flip[pl.ds(1, parts, stride=2), :], 64, 1),
        )

    adj = 5
    pack2([i0[0], i0[adj + 7]], s_1, 0)
    for t, table in enumerate((isrc, idst, iwgt)):
        row = jnp.concatenate([table[0:1, :].astype(F32), table[1:2, :].astype(F32)], axis=1)
        s_t[t : t + 1, :] = row
    pack4([i0[1], i0[2], i0[3], i0[4]], s_2, 0)
    pack2([ext[0, MOD, core], i0[adj + 6]], s_2, 2)
    pack4([ext[0, QW, core], ext[0, QW + 1, core], ext[0, QW + 2, core], i0[adj + 5]], s_q, 0)
    pack2([i0[adj + 4], i0[adj + 3]], s_b, 0)
    pack2([i0[adj + 2], i0[adj + 1]], s_c, 0)
    pack2([i0[adj], zero], s_c, 1)

    for t in range(SENT // 4):
        tile = ext[0, 4 * t : 4 * t + 4, core, :].reshape(128, 128).T
        s_col[0, t] = tile[0:EDGE]
        s_col[1, t] = tile[128 - EDGE :]

    pl.semaphore_wait(barrier, guests)

    def spread(source, target, rows, which, by_pos):
        def send(t, carry):
            peer = far(t)
            take = turn_pos(snake(g, peer)) if by_pos else peer
            land = d if by_pos else pos
            pltpu.make_async_remote_copy(
                src_ref=source.at[pl.ds(pl.multiple_of(take * 8, 8), rows), :],
                dst_ref=target.at[pl.ds(pl.multiple_of(land * 8, 8), rows), :],
                send_sem=bulk_send.at[which],
                recv_sem=bulk_recv.at[which],
                device_id=(g, peer),
                device_id_type=MESH,
            ).start()
            return carry

        lax.fori_loop(0, last, send, 0)
        mine = pl.ds(pl.multiple_of((pos if by_pos else d) * 8, 8), 8)
        here = pl.ds(pl.multiple_of((d if by_pos else pos) * 8, 8), 8)
        target[here, :] = source[mine, :]

    def bulk(source, target, rows, which):
        return pltpu.make_async_remote_copy(
            src_ref=source.at[pl.ds(0, last * rows), :],
            dst_ref=target.at[pl.ds(0, last * rows), :],
            send_sem=bulk_send.at[which],
            recv_sem=bulk_recv.at[which],
            device_id=(g, lax.rem(d + 1, parts)),
            device_id_type=MESH,
        )

    def start_all(copies):
        for cond, copy, _ in copies:
            pl.when(cond)(copy.start)

    def recv_all(copies):
        for _, copy, cond in copies:
            pl.when(cond)(copy.wait_recv)

    def sent_all(copies):
        for cond, copy, _ in copies:
            pl.when(cond)(copy.wait_send)

    halo1 = []
    for at, (away, step, there) in enumerate(beside):
        side, back = (away + 1) // 2, len(beside) - 1 - at
        halo1.append(
            (
                there,
                pltpu.make_async_remote_copy(
                    src_ref=s_col.at[side],
                    dst_ref=r_col.at[1 - side, 1 - step],
                    send_sem=col_send.at[at],
                    recv_sem=col_recv.at[back],
                    device_id=(g + away, d + step),
                    device_id_type=MESH,
                ),
                beside[back][2],
            )
        )
    planes = pl.ds(0, SENT)
    for at, (step, there, source, target, other) in enumerate(
        ((-1, at_top, EDGE, EDGE + 32, at_end), (1, at_end, 32, 0, at_top))
    ):
        halo1.append(
            (
                there,
                pltpu.make_async_remote_copy(
                    src_ref=ext.at[0, planes, pl.ds(source, EDGE)],
                    dst_ref=ext.at[0, planes, pl.ds(target, EDGE)],
                    send_sem=row_send.at[at],
                    recv_sem=row_recv.at[at],
                    device_id=(g, d + step),
                    device_id_type=MESH,
                ),
                other,
            )
        )

    lines, depth = parts // RUN, 3
    line, spot = lax.div(d, RUN), lax.rem(d, RUN)
    slab = pl.ds(pl.multiple_of(spot * 8, 8), depth)

    def along(t, carry):
        half = lax.div(t + 1, 2)
        step = jnp.where(lax.rem(t, 2) == 1, half, -half)
        peer = lax.rem(line + lines // 2 + step, lines)
        pltpu.make_async_remote_copy(
            src_ref=s_t.at[pl.ds(0, depth)],
            dst_ref=r_t.at[line, slab],
            send_sem=tab_send.at[0],
            recv_sem=tab_recv.at[0],
            device_id=(g, peer * RUN + spot),
            device_id_type=MESH,
        ).start()
        return carry

    across = [
        pltpu.make_async_remote_copy(
            src_ref=r_t.at[:, slab],
            dst_ref=r_t.at[:, slab],
            send_sem=tab_send.at[step],
            recv_sem=tab_recv.at[step],
            device_id=(g, line * RUN + lax.rem(spot + step, RUN)),
            device_id_type=MESH,
        )
        for step in range(1, RUN)
    ]
    tables = pltpu.make_async_remote_copy(
        src_ref=r_t.at[pl.ds(0, lines - 1), pl.ds(0, depth)],
        dst_ref=r_t.at[pl.ds(0, lines - 1), pl.ds(0, depth)],
        send_sem=tab_send.at[0],
        recv_sem=tab_recv.at[0],
        device_id=(g, lax.rem(d + 1, parts)),
        device_id_type=MESH,
    )

    lax.fori_loop(0, lines - 1, along, 0)
    r_t[line, slab, :] = s_t[0:depth, :]
    spread(s_1, r_1, 1, 0, True)
    spread(s_2, r_2, 3, 1, True)
    spread(s_q, r_q, 2, 5, True)
    spread(s_b, r_b, 1, 2, True)

    def unpack(source, first, second):
        return jnp.concatenate(
            [
                source[pl.ds(first, parts, stride=8), :],
                source[pl.ds(second, parts, stride=8), :],
            ],
            axis=0,
        ).T

    def halo0(slot):
        return (
            (
                at_left,
                pltpu.make_async_remote_copy(
                    src_ref=s_l.at[slot],
                    dst_ref=f_r.at[slot],
                    send_sem=side_send.at[slot, 0],
                    recv_sem=side_recv.at[slot, 1],
                    device_id=left,
                    device_id_type=MESH,
                ),
                at_right,
            ),
            (
                at_right,
                pltpu.make_async_remote_copy(
                    src_ref=s_r.at[slot],
                    dst_ref=f_l.at[slot],
                    send_sem=side_send.at[slot, 1],
                    recv_sem=side_recv.at[slot, 0],
                    device_id=right,
                    device_id_type=MESH,
                ),
                at_left,
            ),
        )

    def show(slot, x, v):
        s_l[slot] = jnp.where(low, x, pltpu.roll(v, 64, 1))
        s_r[slot] = jnp.where(low, pltpu.roll(x, 64, 1), v)
        start_all(halo0(slot))

    def unpack2(source, row):
        both = unpack(source, row, row)
        return [jnp.where(low, both[at : at + 32], both[at + 64 : at + 96]) for at in (0, 32)]

    tables.wait_recv()
    for copy in across:
        copy.start()
    bulk(s_1, r_1, 1, 0).wait_recv()
    x, v = unpack2(r_1, 0)
    v = STEP_SQ * v
    show(0, x, v)
    xp[8:40, :] = x
    vp[8:40, :] = v
    vel0[STEPS - 1] = v
    vold[...] = zero
    for l in range(SLS):
        p0[l] = zero

    for copy in across:
        copy.wait()
    flat[...] = r_t[...].reshape(parts * 8, 128)
    src[...] = unpack(flat, 0, 0)
    dst[...] = unpack(flat, 1, 1)
    wgt[...] = unpack(flat, 2, 2)
    bulk(s_2, r_2, 3, 1).wait_recv()
    four = unpack(r_2, 0, 1)
    xold[...] = four[0:32]
    for l in range(SLS):
        m0[l] = four[32 + 32 * l : 64 + 32 * l]
    mod0[...], adj0[6] = unpack2(r_2, 2)

    def swap(a):
        t = a.T
        top, bottom = t[0:64], t[64:128]
        half = wide[0:64]
        return jnp.concatenate(
            [
                jnp.where(half, top, pltpu.roll(bottom, 64, 1)),
                jnp.where(half, pltpu.roll(top, 64, 1), bottom),
            ],
            axis=0,
        )

    def pick(table, plane):
        rows = table[...]
        out = jnp.zeros((128, 128), F32)
        for r in range(32):
            out = jnp.where(rows == float(r), plane[8 + r : 9 + r, :], out)
        return out

    def drop(table, values, out):
        rows = table[...]
        for r in range(32):
            out[r : r + 1, :] = jnp.sum(
                jnp.where(rows == float(r), values, 0.0), axis=0, keepdims=True
            )

    part = lax.rem(lax.broadcasted_iota(jnp.int32, (1, 128), 1), 64)

    def rims(plane):
        plane[7:8, :] = jnp.where(part == 0, 0.0, pltpu.roll(plane[39:40, :], 1, 1))
        plane[40:41, :] = jnp.where(part == 63, 0.0, pltpu.roll(plane[8:9, :], 127, 1))

    def ready(now, old, kept, other, turned_now, plane):
        own = plane[9:41, :] + plane[7:39, :] + turned_now - 4.0 * now
        rest = 2.0 * now - old + STEP_SQ * (other - (kept[0] + kept[1] + kept[2]))
        return own, rest

    def absorb(k, adjoint):
        for l in range(SLS):
            mem0[k - 1, l] = m0[l]
            m0[l] = RELAX[l] * m0[l] + q0[l] * fx[...]
            if adjoint:
                p0[l] = RELAX[l] * p0[l] + q0[l] * fv[...]

    def round0(k, adjoint):
        slot = lax.rem(k, 2)
        copies = halo0(slot)
        drop(dst, swap(pick(src, xp)) * wgt[...], cx)
        rims(xp)
        if adjoint:
            drop(src, swap(pick(dst, vp) * wgt[...]), cv)
            rims(vp)
        if adjoint:

            @pl.when(k == 1)
            def _():
                bulk(s_q, r_q, 2, 5).wait_recv()
                four = unpack(r_q, 0, 1)
                for l in range(SLS):
                    q0[l] = four[32 * l : 32 * l + 32]
                adj0[5] = four[96:128]

            @pl.when(k > 0)
            def _():
                absorb(k, True)

        x = xp[8:40, :]
        m = [m0[l] for l in range(SLS)]
        x_own, x_rest = ready(x, xold[...], m, cx[...], pltpu.roll(x, 64, 1), xp)
        if adjoint:

            @pl.when(k == 2)
            def _():
                bulk(s_b, r_b, 1, 2).wait_recv()
                adj0[4], adj0[3] = unpack2(r_b, 0)

            @pl.when(k == 4)
            def _():
                bulk(s_c, r_c, 2, 6).wait_recv()
                adj0[2], adj0[1] = unpack2(r_c, 0)
                adj0[0] = unpack2(r_c, 1)[0]

            n = STEPS - 2 - k
            v = vp[8:40, :]
            p = [p0[l] for l in range(SLS)]
            v_own, v_rest = ready(v, vold[...], p, cv[...] + adj0[n], pltpu.roll(v, 64, 1), vp)
        recv_all(copies)
        from_l, from_r = f_l[slot], f_r[slot]
        lap = x_own + jnp.where(low, from_l, pltpu.roll(from_r, 64, 1))
        force = mod0[...] * lap
        fresh = x_rest + STEP_SQ * force
        if adjoint:
            v_force = mod0[...] * (v_own + jnp.where(low, pltpu.roll(from_l, 64, 1), from_r))
            v_fresh = v_rest + STEP_SQ * v_force
            show(1 - slot, fresh, v_fresh)
        lap0[k] = lap
        xold[...] = x
        xp[8:40, :] = fresh
        if adjoint:
            fx[...] = force
            fv[...] = v_force
            vold[...] = v
            vp[8:40, :] = v_fresh
            vel0[n] = v_fresh
        sent_all(copies)

    def step0(k, carry):
        @pl.when(k == 1)
        def _():
            spread(s_c, r_c, 2, 6, True)

        @pl.when(k == 4)
        def _():
            start_all(halo1)

        round0(k, True)
        return carry

    lax.fori_loop(0, STEPS - 1, step0, 0)
    absorb(STEPS - 1, False)

    def terms(vel, lap, mem, count):
        mu = zero
        q = [zero] * SLS
        for n in range(count):
            mu = mu + vel(n) * lap(n)
            for l in range(SLS):
                q[l] = q[l] + vel(n) * mem(n, l)
        return mu, q

    mu, _ = terms(lambda n: vel0[n], lambda n: lap0[n], lambda n, l: zero, STEPS - 1)
    q = [zero] * SLS
    for n in range(STEPS):
        for l in range(SLS):
            q[l] = q[l] + vel0[n] * (mem0[n, l] if n < STEPS - 1 else m0[l])
    turn = jnp.concatenate([mu] + q, axis=0).T
    s_o[pl.ds(0, parts, stride=8), :] = turn[0:64]
    s_o[pl.ds(1, parts, stride=8), :] = turn[64:128]
    spread(s_o, r_o, 2, 3, False)

    round0(STEPS - 1, False)

    turn = jnp.concatenate([xp[8:40, :], vel0[STEPS - 1] * lap0[STEPS - 1], zero, zero], axis=0).T
    s_e[pl.ds(0, parts, stride=8), :] = jnp.where(
        wide[0:64], turn[0:64], pltpu.roll(turn[64:128], 64, 1)
    )
    spread(s_e, r_e, 1, 4, False)

    recv_all(halo1)
    inner = lax.rem(lax.broadcasted_iota(jnp.int32, (EDGE, 128), 1), 32) < 16
    blank = jnp.zeros((128 - 2 * EDGE, 128), F32)

    def beside_planes(tiles):
        return jnp.concatenate([tiles[1], blank, tiles[0]], axis=0).T.reshape(4, 32, 128)

    for t in range(SENT // 4):
        four = slice(4 * t, 4 * t + 4)
        ext[1, four, core, :] = beside_planes([r_col[side, 1, t] for side in range(2)])
        ends = beside_planes(
            [jnp.where(inner, r_col[side, 2, t], r_col[side, 0, t]) for side in range(2)]
        )
        ext[1, four, 0:EDGE, :] = ends[:, 32 - EDGE :, :]
        ext[1, four, EDGE + 32 : 2 * EDGE + 32, :] = ends[:, 0:EDGE, :]
    sent_all(halo1)
    for c in range(2):
        for t in range(2):
            zp[c, t, 8:56, :] = ext[t, NOW + c]
            zp[c + 2, t, 8:56, :] = STEP_SQ * ext[t, ADJ + c]
            zold[c, t] = ext[t, PREV + c]
        vel1[STEPS, c] = STEP_SQ * ext[0, ADJ + c, core, :]

    rim = lax.broadcasted_iota(jnp.int32, (48, 128), 1)

    def around(f):
        main, side = zp[f, 0, 8:56, :], zp[f, 1, 8:56, :]
        lap = []
        ahead = [pltpu.roll(a, 127, 1) for a in (main, side)]
        behind = [pltpu.roll(a, 1, 1) for a in (main, side)]
        for t, centre in enumerate((main, side)):
            lap.append(
                zp[f, t, 9:57, :]
                + zp[f, t, 7:55, :]
                + jnp.where(rim == 127, ahead[1 - t], ahead[t])
                + jnp.where(rim == 0, behind[1 - t], behind[t])
                - 4.0 * centre
            )
        return (main, side), lap

    def round1(k, carry):
        n = STEPS - 2 - k
        source = ADJ + 2 * jnp.minimum(k + 1, STEPS - 1)
        for c in range(2):
            now, lap = around(c)
            lap1[k, c] = lap[0][8:40]
            for l in range(SLS):
                mem1[k, l, c] = ext[0, MEM + 2 * l + c, core, :]
            for t in range(2):
                kept = [ext[t, MEM + 2 * l + c] for l in range(SLS)]
                force = ext[t, MOD] * lap[t]
                accel = force - (kept[0] + kept[1] + kept[2])
                fresh = 2.0 * now[t] - zold[c, t] + STEP_SQ * accel
                for l in range(SLS):
                    ext[t, MEM + 2 * l + c] = RELAX[l] * kept[l] + ext[t, QW + l] * force
                zold[c, t] = now[t]
                zp[c, t, 8:56, :] = fresh
            now, lap = around(c + 2)
            for t in range(2):
                kept = [p1[l, c, t] for l in range(SLS)]
                force = ext[t, MOD] * lap[t]
                accel = force - (kept[0] + kept[1] + kept[2]) + ext[t, source + c]
                fresh = 2.0 * now[t] - zold[c + 2, t] + STEP_SQ * accel
                for l in range(SLS):
                    p1[l, c, t] = RELAX[l] * kept[l] + ext[t, QW + l] * force
                zold[c + 2, t] = now[t]
                zp[c + 2, t, 8:56, :] = fresh
                if t == 0:
                    vel1[n + 1, c] = fresh[8:40]
        return carry

    lax.fori_loop(0, STEPS, round1, 0)

    mu_sum, q_sum = zero, [zero] * SLS
    for c in range(2):
        o_u[c + 1] = zp[c, 0, 16:48, :]
        mu, q = terms(
            lambda n: vel1[n + 1, c], lambda n: lap1[n, c], lambda n, l: mem1[n, l, c], STEPS
        )
        mu_sum = mu_sum + mu
        q_sum = [a + b for a, b in zip(q_sum, q)]
    o_mu[...] = mu_sum
    for l in range(SLS):
        o_q[l] = q_sum[l]

    bulk(s_o, r_o, 2, 3).wait_recv()
    flip[pl.ds(0, parts, stride=2), :] = r_o[pl.ds(0, parts, stride=8), :]
    flip[pl.ds(1, parts, stride=2), :] = r_o[pl.ds(1, parts, stride=8), :]
    four = flip[...].T
    scale = 1.0 / (3.0 * STEPS)
    mu = o_mu[...] + four[0:32]
    for l in range(SLS):
        o_q[l] = (o_q[l] + four[32 + 32 * l : 64 + 32 * l]) * scale
    bulk(s_e, r_e, 1, 4).wait_recv()
    ends = r_e[pl.ds(0, parts, stride=8), :]
    flip[pl.ds(0, parts, stride=2), :] = ends
    flip[pl.ds(1, parts, stride=2), :] = pltpu.roll(ends, 64, 1)
    four = flip[...].T
    o_u[0] = four[0:32]
    o_mu[...] = (mu + four[32:64]) * scale

    bulk(s_1, r_1, 1, 0).wait_send()
    bulk(s_2, r_2, 3, 1).wait_send()
    bulk(s_q, r_q, 2, 5).wait_send()
    bulk(s_b, r_b, 1, 2).wait_send()
    bulk(s_c, r_c, 2, 6).wait_send()
    tables.wait_send()
    bulk(s_o, r_o, 2, 3).wait_send()
    bulk(s_e, r_e, 1, 4).wait_send()


def solution(mesh):
    groups, parts = mesh.shape["group"], mesh.shape["dom"]

    def shards(
        u_prev, u_now, memory, modulus, q_weight, adjoint_source, couple_src, couple_dst, couple_weight
    ):
        tables = [t.reshape(parts, -1).T for t in (couple_src, couple_dst, couple_weight)]
        plane = (32, 128)
        square = (128, 128)

        def vmem(*shape):
            return pltpu.VMEM(shape, F32)

        dma = pltpu.SemaphoreType.DMA
        return pl.pallas_call(
            functools.partial(kernel, groups, parts),
            out_shape=(vmem(*u_now.shape), vmem(*modulus.shape), vmem(*q_weight.shape)),
            in_specs=[pl.BlockSpec(memory_space=pltpu.HBM)] * 9,
            out_specs=[pl.BlockSpec(memory_space=pltpu.VMEM)] * 3,
            scratch_shapes=[
                vmem(5 + STEPS, *plane),
                pltpu.VMEM((2, parts), jnp.int32),
                pltpu.VMEM((2, parts), jnp.int32),
                vmem(2, parts),
                vmem(*square),
            ]
            + [vmem(parts * 8, 128)] * 10
            + [vmem(8, 128), vmem(parts // RUN, RUN * 8, 128)]
            + [vmem(parts * 8, 128)] * 5
            + [
                vmem(*square),
                vmem(*square),
                vmem(*square),
                vmem(*plane),
                vmem(SLS, *plane),
                vmem(STEPS - 1, *plane),
                vmem(48, 128),
                vmem(48, 128),
                vmem(*plane),
                vmem(*plane),
                vmem(SLS, *plane),
                vmem(SLS, *plane),
                vmem(*plane),
                vmem(*plane),
                vmem(*plane),
                vmem(*plane),
                vmem(STEPS, *plane),
                vmem(STEPS, *plane),
                vmem(STEPS, SLS, *plane),
                vmem(2, *plane),
                vmem(2, *plane),
                vmem(2, *plane),
                vmem(2, *plane),
                vmem(2, SENT + 2, 48, 128),
                vmem(4, 2, 64, 128),
                vmem(4, 2, 48, 128),
                vmem(SLS, 2, 2, 48, 128),
                vmem(STEPS, 2, *plane),
                vmem(STEPS + 1, 2, *plane),
                vmem(STEPS, SLS, 2, *plane),
                vmem(2, SENT // 4, EDGE, 128),
                vmem(2, 3, SENT // 4, EDGE, 128),
                dma((22,)),
                dma((7,)),
                dma((7,)),
                dma((2, 2)),
                dma((2, 2)),
                dma((6,)),
                dma((6,)),
                dma((2,)),
                dma((2,)),
                dma((RUN,)),
                dma((RUN,)),
            ],
            compiler_params=pltpu.CompilerParams(
                collective_id=0, has_side_effects=True, vmem_limit_bytes=60 * 1024 * 1024
            ),
        )(u_prev, u_now, memory, modulus, q_weight, adjoint_source, *tables)

    in_specs = (
        P(None, "dom", "group"),
        P(None, "dom", "group"),
        P(None, None, "dom", "group"),
        P("dom", "group"),
        P(None, "dom", "group"),
        P(None, None, "dom", "group"),
        P("group", "dom", None, None),
        P("group", "dom", None, None),
        P("group", "dom", None, None),
    )
    out_specs = (P(None, "dom", "group"), P("dom", "group"), P(None, "dom", "group"))
    return jax.shard_map(shards, mesh=mesh, in_specs=in_specs, out_specs=out_specs, check_vma=False)
```
